32 devices in a mesh: groups: 2 (over x), node: 2 (over core), local: 8 (over z, y).
Axes of the slice: x: 2, y: 2, z: 4, core: 2. Of those that a mesh axis runs over, the one named last changes fastest.
Arguments:
- grad_out: bfloat16 [4096, 4096], P(('groups', 'node', 'local')), parts along dimension 0, may hold values from -6 to 6
- layer_in: bfloat16 [4096, 4096], P(('groups', 'node', 'local')), parts along dimension 0, may hold values from -6 to 6
- expert_ids: int32 [4096, 8], P(('groups', 'node', 'local')), parts along dimension 0, may hold values from 0 to 127, all different within a row; in each aligned block of 128 rows (0 to 127, 128 to 255, ...) at most 16 rows name the same one
- gate_probs: float32 [4096, 8], P(('groups', 'node', 'local')), parts along dimension 0, may hold values from 0.1 to 0.6
- sample_ids: int32 [32, 128], P(('groups', 'node', 'local')), parts along dimension 0, may hold values from 0 to 7, never falling along the last dimension, each value on 1 to 64 neighbouring positions
- w_gate: bfloat16 [3072, 4096], P(('node', 'local')), may hold values from -0.09375 to 0.09375
- w_up: bfloat16 [3072, 4096], P(('node', 'local')), may hold values from -0.09375 to 0.09375
- w_down: bfloat16 [3072, 4096], P(('node', 'local')), may hold values from -0.15625 to 0.15625
Outputs:
- grad_in: bfloat16 [4096, 4096], P(('groups', 'node', 'local')), parts along dimension 0
- grad_gate: bfloat16 [6144, 4096], P(('groups', 'node', 'local')), parts along dimension 0
- grad_up: bfloat16 [6144, 4096], P(('groups', 'node', 'local')), parts along dimension 0
- grad_down: bfloat16 [6144, 4096], P(('groups', 'node', 'local')), parts along dimension 0
The draws below stay inside these ranges and needn't reach their ends.
There are 2 independent parts, one for each index of `groups`. The reference program is written for one: setup_inputs(seed, part) draws one part's arguments, and reference() takes and returns one part's arrays. A program takes and returns all parts, laid end to end along the dimension named above; an argument that names none is the same for every part. Nothing has to cross between parts.
Inputs may be any that keep to these rules, and one draw needn't show every extreme that they name: `expert_ids`: in each aligned block of 128 rows (the rows of one device) no expert is named by more than 16 rows, and one expert is named by exactly 16 rows; the numbers in a row differ. `sample_ids`: each packed row holds 8 samples numbered in order, never falling, each of 1 to 64 positions; one sample is exactly that long.
All inputs are finite; a program needn't handle non-finite values.
Results may differ from the reference program's by a relative error of at most 0.0066.
Values may be sent and summed in bfloat16 or wider, within the bound.
No kernel may reach another device: no remote copies, remote signals or barrier semaphores. Data moves between devices by JAX's collectives and lax.ppermute only.
A program may use at most 128 MiB of HBM per device.

```python
import math
import jax
import jax.numpy as jnp
import numpy as np
from jax import lax

D = 4096
FF = 1536
EXPERTS = 128
TOP = 8
HID_DEV = 192
SAMPLES = 8
TOK_DEV = 128
CAP = 16
WAVE = 2
PACKS = 16
TOKENS = 2048


def levels(key, dims, cuts, least, largest):
    factor_of = 1.0
    for dim, parts in cuts:
        heights = jax.random.uniform(jax.random.fold_in(jax.random.fold_in(key, 6), dim), (parts,), jnp.float32, least / len(cuts), largest / len(cuts))
        factor_of = factor_of * jnp.repeat(jnp.exp(heights), dims[dim] // parts).reshape((-1,) + (1,) * (len(dims) - 1 - dim))
    return factor_of


def split_up(amount, total, limit, skew):
    portions = [(1 << 20) // math.isqrt(rank ** skew) + 1 for rank in range(2, amount + 1)]
    rest, holding = total - limit - (amount - 1), [1] * (amount - 1)
    while rest > 0:
        movable = [i for i in range(amount - 1) if holding[i] < limit]
        mass, budget = sum([portions[i] for i in movable]), rest
        for i in movable:
            extra = min(limit - holding[i], max(1, budget * portions[i] // mass), rest)
            holding[i] = holding[i] + extra
            rest = rest - extra
    return np.array([limit] + holding)


def ragged(own_key, number_of, total, bound, skew):
    if number_of == 2:
        one = jax.random.randint(own_key, (), max(1, total - bound), min(bound, total - 1) + 1)
        return jnp.stack([one, total - one])
    lengths = jnp.asarray(split_up(number_of, total, bound, skew), jnp.int32)
    couples = (number_of - 1) // 2
    source_of, receiver = lengths[1:1 + 2 * couples:2], lengths[2:2 + 2 * couples:2]
    room = jnp.minimum(source_of - 1, bound - receiver)
    passed = jax.random.randint(jax.random.fold_in(own_key, 1), (couples,), 0, 1 << 20) % (room + 1)
    lengths = lengths.at[1:1 + 2 * couples:2].set(source_of - passed).at[2:2 + 2 * couples:2].set(receiver + passed)
    return lengths[jax.random.permutation(jax.random.fold_in(own_key, 2), number_of)]


def assign_block(stream_key, own, number, rows, number_of, top, limit, skew):
    sequence = jax.random.permutation(stream_key, number_of)
    crowded, ordinary = portions_of(number_of, rows * top, limit, skew, True), portions_of(number_of, rows * top, limit, skew, False)
    places = jnp.arange(number_of)

    def named(sizes, offset_by):
        used = int((sizes > 0).sum())
        fixed = max(1, used // 4)
        moved = fixed + (places - fixed + offset_by * (used - fixed)) % max(1, number_of - fixed)
        return jnp.zeros((number_of,), jnp.int32).at[sequence[jnp.where(places < fixed, places, moved)]].set(jnp.asarray(sizes, jnp.int32))

    sizes = jnp.where(number % 4 == 0, named(crowded, number // 4), named(ordinary, number - number // 4 - 1))
    mixed = jax.random.permutation(jax.random.fold_in(own, 3), number_of)
    source_of, taker = mixed[0:number_of // 2 * 2:2], mixed[1:number_of // 2 * 2:2]
    room = jnp.minimum(sizes[source_of] - 1, limit - sizes[taker]) // 2
    room = jnp.where((source_of == sequence[0]) | (taker == sequence[0]) | (sizes[taker] == 0), 0, jnp.maximum(room, 0))
    moved = jax.random.randint(jax.random.fold_in(own, 4), (number_of // 2,), 0, 1 << 20) % (room + 1)
    sizes = sizes.at[source_of].add(-moved).at[taker].add(moved)
    labels = jnp.searchsorted(jnp.cumsum(sizes), jnp.arange(rows * top), side="right").astype(jnp.int32)
    listing = labels.reshape(top, rows).T
    listing = listing[jax.random.permutation(jax.random.fold_in(own, 1), rows)]
    offset_by = jax.random.randint(jax.random.fold_in(own, 2), (rows, 1), 0, top)
    return jnp.take_along_axis(listing, (jnp.arange(top)[None, :] + offset_by) % top, axis=1)


def portions_of(amount, total, limit, skew, full):
    loads = [(1 << 20) // math.isqrt(rank ** skew) + 1 for rank in range(1, amount + 1)]
    largest = limit if full else min(limit, max(-(-total // amount), total * loads[0] // sum(loads)))
    least = 1 if total - largest >= amount - 1 else 0
    counts, surplus = [largest] + [least] * (amount - 1), total - largest - least * (amount - 1)
    while surplus > 0:
        movable = [i for i in range(1, amount) if counts[i] < largest] or [i for i in range(1, amount) if counts[i] < limit]
        whole, remaining = sum([loads[i] for i in movable]), surplus
        for i in movable:
            more = min(limit - counts[i], max(1, remaining * loads[i] // whole), surplus)
            counts[i] = counts[i] + more
            surplus = surplus - more
    return np.array(counts)


def normal_values(rng, dims, spread, most, cuts=(), held_as=jnp.bfloat16):
    entries = jax.random.normal(rng, dims, jnp.float32) * spread
    if len(cuts) > 0:
        entries = levels(rng, dims, cuts, -0.22, 0.18) * entries
    return jnp.clip(entries, min=-most, max=most).astype(held_as)


def setup_inputs(seed: int = 0, part: int = 0) -> dict:
    arg_keys = jax.random.split(jax.random.key(seed), 9)
    own_keys = jax.random.split(jax.random.fold_in(arg_keys[8], part), 9)
    grad_out = normal_values(own_keys[0], (TOKENS, D), 1.0, 6.0, ((0, 16),))
    layer_in = normal_values(own_keys[1], (TOKENS, D), 1.0, 6.0, ((0, 16),))
    expert_ids_keys = jax.random.split(jax.random.fold_in(own_keys[2], 1), TOKENS // TOK_DEV)
    expert_ids_turns = jax.random.permutation(jax.random.fold_in(own_keys[2], 3), TOKENS // TOK_DEV)
    expert_ids = jax.vmap(lambda own, number: assign_block(jax.random.fold_in(own_keys[2], 2), own, number, TOK_DEV, EXPERTS, TOP, CAP, 1))(expert_ids_keys, expert_ids_turns).reshape((TOKENS, TOP))
    gate_probs = jnp.clip(0.1 + 0.5 * jax.random.uniform(own_keys[3], (TOKENS, TOP), jnp.float32) ** levels(own_keys[3], (TOKENS, TOP), ((0, 16),), -0.2, 0.2), 0.1, 0.6)
    sample_ids = jax.vmap(lambda own: jnp.searchsorted(jnp.cumsum(ragged(own, SAMPLES, TOK_DEV, TOK_DEV // 2, 1)), jnp.arange(TOK_DEV), side="right"))(jax.random.split(own_keys[4], PACKS)).reshape((PACKS, TOK_DEV)).astype(jnp.int32)
    w_gate = normal_values(arg_keys[5], (WAVE * FF, D), D ** -0.5, 0.09375, ((0, 16),))
    w_up = normal_values(arg_keys[6], (WAVE * FF, D), D ** -0.5, 0.09375, ((0, 16),))
    w_down = normal_values(arg_keys[7], (WAVE * FF, D), FF ** -0.5, 0.15625, ((0, 16),))
    return dict(grad_out=grad_out, layer_in=layer_in, expert_ids=expert_ids, gate_probs=gate_probs, sample_ids=sample_ids, w_gate=w_gate, w_up=w_up, w_down=w_down)


def silu_parts(pre):
    sigma = jax.nn.sigmoid(pre)
    return pre * sigma, sigma * (1.0 + pre * (1.0 - sigma))


def expert_backward(rows_grad, rows_in, gate_rows, up_rows, down_rows):
    contract = (((1,), (1,)), ((), ()))
    over_rows = (((0,), (0,)), ((), ()))
    gate_pre = lax.dot_general(rows_in, gate_rows, contract, preferred_element_type=jnp.float32)
    up_pre = lax.dot_general(rows_in, up_rows, contract, preferred_element_type=jnp.float32)
    d_act = lax.dot_general(rows_grad, down_rows, contract, preferred_element_type=jnp.float32)
    act, slope = silu_parts(gate_pre)
    hidden = (act * up_pre).astype(jnp.bfloat16)
    d_up = (d_act * act).astype(jnp.bfloat16)
    d_gate = (d_act * up_pre * slope).astype(jnp.bfloat16)
    g_down = lax.dot_general(hidden, rows_grad, over_rows, preferred_element_type=jnp.float32).astype(jnp.bfloat16)
    g_gate = lax.dot_general(d_gate, rows_in, over_rows, preferred_element_type=jnp.float32).astype(jnp.bfloat16)
    g_up = lax.dot_general(d_up, rows_in, over_rows, preferred_element_type=jnp.float32).astype(jnp.bfloat16)
    return d_gate, d_up, g_gate, g_up, g_down


def reference(grad_out, layer_in, expert_ids, gate_probs, sample_ids, w_gate, w_up, w_down):
    packs = TOKENS // TOK_DEV
    shards = FF // HID_DEV
    same_sample = sample_ids[:, :, None] == sample_ids[:, None, :]
    length = jnp.sum(same_sample.astype(jnp.int32), axis=2)
    loss_scale = (TOK_DEV / (SAMPLES * length.astype(jnp.float32))).reshape(TOKENS)
    slot_range = jnp.arange(CAP, dtype=jnp.int32)
    position = jnp.arange(TOK_DEV, dtype=jnp.int32)
    pack_start = jnp.arange(packs, dtype=jnp.int32)[:, None] * TOK_DEV
    total = jnp.zeros((TOKENS, D), jnp.float32)
    grads_gate = []
    grads_up = []
    grads_down = []
    for expert in range(WAVE):
        hit = expert_ids == expert
        coef = jnp.sum(jnp.where(hit, gate_probs, 0.0), axis=1)
        member = jnp.any(hit, axis=1).reshape(packs, TOK_DEV).astype(jnp.int32)
        rank = jnp.cumsum(member, axis=1) - 1
        picked = (member[:, :, None] == 1) & (rank[:, :, None] == slot_range[None, None, :])
        local_pos = jnp.sum(jnp.where(picked, position[None, :, None], 0), axis=1).astype(jnp.int32)
        valid = jnp.any(picked, axis=1).reshape(-1)
        where_rows = (local_pos + pack_start).reshape(-1).astype(jnp.int32)
        factor = jnp.where(valid, coef[where_rows] * loss_scale[where_rows], 0.0)
        rows_grad = (factor[:, None] * grad_out[where_rows].astype(jnp.float32)).astype(jnp.bfloat16)
        rows_in = jnp.where(valid[:, None], layer_in[where_rows], jnp.zeros((), jnp.bfloat16)).astype(jnp.bfloat16)
        gate_rows = lax.dynamic_slice_in_dim(w_gate, expert * FF, FF, 0)
        up_rows = lax.dynamic_slice_in_dim(w_up, expert * FF, FF, 0)
        down_rows = lax.dynamic_slice_in_dim(w_down, expert * FF, FF, 0)
        d_gate, d_up, g_gate, g_up, g_down = expert_backward(rows_grad, rows_in, gate_rows, up_rows, down_rows)
        grads_gate.append(g_gate)
        grads_up.append(g_up)
        grads_down.append(g_down)
        count = d_gate.shape[0]
        dg_blocks = d_gate.astype(jnp.float32).reshape(count, shards, HID_DEV)
        du_blocks = d_up.astype(jnp.float32).reshape(count, shards, HID_DEV)
        wg_blocks = gate_rows.astype(jnp.float32).reshape(shards, HID_DEV, D)
        wu_blocks = up_rows.astype(jnp.float32).reshape(shards, HID_DEV, D)
        pieces = jnp.einsum("rsh,shd->rsd", dg_blocks, wg_blocks) + jnp.einsum("rsh,shd->rsd", du_blocks, wu_blocks)
        rounded = lax.optimization_barrier(pieces.astype(jnp.bfloat16))
        summed = jnp.sum(rounded.astype(jnp.float32), axis=1)
        total = total.at[where_rows].add(jnp.where(valid[:, None], summed, 0.0))
    grad_in = total.astype(jnp.bfloat16)
    grad_gate = jnp.concatenate(grads_gate, axis=0)
    grad_up = jnp.concatenate(grads_up, axis=0)
    grad_down = jnp.concatenate(grads_down, axis=0)
    return (grad_in, grad_gate, grad_up, grad_down)
```

```python
import jax
import jax.numpy as jnp
from jax import lax
from jax.sharding import PartitionSpec as P

FF = 1536
SAMPLES = 8
TOK_DEV = 128
CAP = 16


def silu_parts(pre):
    sigma = jax.nn.sigmoid(pre)
    return (pre * sigma, sigma * (1.0 + pre * (1.0 - sigma)))


def per_device_exchange(grad_out, layer_in, expert_ids, gate_probs, sample_ids, w_gate, w_up, w_down):
    tok_count = grad_out.shape[0]
    width = grad_out.shape[1]
    shard_width = w_gate.shape[0]
    node_count = lax.axis_size("node")
    local_count = lax.axis_size("local")
    devices = node_count * local_count
    shards = FF // shard_width
    wave = devices // shards
    contract = (((1,), (1,)), ((), ()))
    over_rows = (((0,), (0,)), ((), ()))
    packed = sample_ids[0]
    same_sample = packed[:, None] == packed[None, :]
    length = jnp.sum(same_sample.astype(jnp.int32), axis=1)
    loss_scale = TOK_DEV / (SAMPLES * length.astype(jnp.float32))
    expert_range = jnp.arange(wave, dtype=jnp.int32)
    hit = expert_ids[:, :, None] == expert_range[None, None, :]
    coef = jnp.sum(jnp.where(hit, gate_probs[:, :, None], 0.0), axis=1)
    member = jnp.any(hit, axis=1).astype(jnp.int32)
    rank = jnp.cumsum(member, axis=0) - 1
    slot_range = jnp.arange(CAP, dtype=jnp.int32)
    picked = (member[:, :, None] == 1) & (rank[:, :, None] == slot_range[None, None, :])
    factor = coef * loss_scale[:, None]
    slot_factor = jnp.sum(jnp.where(picked, factor[:, :, None], 0.0), axis=0).reshape(wave * CAP, 1)
    select = picked.astype(jnp.bfloat16).reshape(tok_count, wave * CAP)
    chosen_grad = lax.dot_general(select, grad_out, over_rows, preferred_element_type=jnp.float32)
    send_grad = (slot_factor * chosen_grad).astype(jnp.bfloat16)
    send_in = lax.dot_general(
        select, layer_in, over_rows, preferred_element_type=jnp.float32
    ).astype(jnp.bfloat16)
    flat_grad = jnp.broadcast_to(
        send_grad.reshape(wave, 1, CAP, width), (wave, shards, CAP, width)
    ).reshape(devices, CAP, width)
    flat_in = jnp.broadcast_to(
        send_in.reshape(wave, 1, CAP, width), (wave, shards, CAP, width)
    ).reshape(devices, CAP, width)
    recv_grad, recv_in = (
        lax.all_to_all(flat_grad, ("node", "local"), split_axis=0, concat_axis=0, tiled=True),
        lax.all_to_all(flat_in, ("node", "local"), split_axis=0, concat_axis=0, tiled=True),
    )
    rows_grad = recv_grad.reshape(devices * CAP, width)
    rows_in = recv_in.reshape(devices * CAP, width)
    gate_pre = lax.dot_general(rows_in, w_gate, contract, preferred_element_type=jnp.float32)
    up_pre = lax.dot_general(rows_in, w_up, contract, preferred_element_type=jnp.float32)
    d_act = lax.dot_general(rows_grad, w_down, contract, preferred_element_type=jnp.float32)
    act, slope = silu_parts(gate_pre)
    hidden = (act * up_pre).astype(jnp.bfloat16)
    d_up = (d_act * act).astype(jnp.bfloat16)
    d_gate = (d_act * up_pre * slope).astype(jnp.bfloat16)
    grad_down = lax.dot_general(
        hidden, rows_grad, over_rows, preferred_element_type=jnp.float32
    ).astype(jnp.bfloat16)
    grad_gate = lax.dot_general(
        d_gate, rows_in, over_rows, preferred_element_type=jnp.float32
    ).astype(jnp.bfloat16)
    grad_up = lax.dot_general(d_up, rows_in, over_rows, preferred_element_type=jnp.float32).astype(
        jnp.bfloat16
    )
    pieces = jnp.dot(d_gate, w_gate, preferred_element_type=jnp.float32)
    pieces = (pieces + jnp.dot(d_up, w_up, preferred_element_type=jnp.float32)).astype(jnp.bfloat16)
    returned = lax.all_to_all(
        pieces.reshape(devices, CAP, width),
        ("node", "local"),
        split_axis=0,
        concat_axis=0,
        tiled=True,
    )
    returned = returned.reshape(devices * CAP, width)
    select_all = jnp.broadcast_to(
        select.reshape(tok_count, wave, 1, CAP), (tok_count, wave, shards, CAP)
    )
    select_all = select_all.reshape(tok_count, devices * CAP)
    grad_in = jnp.dot(select_all, returned, preferred_element_type=jnp.float32).astype(jnp.bfloat16)
    return (grad_in, grad_gate, grad_up, grad_down)


def ring_orders(count):
    order = list(range(0, count, 2)) + list(range(count - 1, 0, -2))
    ahead = [(order[i], order[(i + 1) % count]) for i in range(count)]
    behind = [(order[i], order[(i - 1) % count]) for i in range(count)]
    return ahead, behind


def per_device_ring(grad_out, layer_in, expert_ids, gate_probs, sample_ids, w_gate, w_up, w_down):
    width = grad_out.shape[1]
    local_count = lax.axis_size("local")
    wave = lax.axis_size("node")
    me = lax.axis_index("node")
    contract = (((1,), (1,)), ((), ()))
    over_rows = (((0,), (0,)), ((), ()))
    packed = sample_ids[0]
    same_sample = packed[:, None] == packed[None, :]
    length = jnp.sum(same_sample.astype(jnp.int32), axis=1)
    loss_scale = TOK_DEV / (SAMPLES * length.astype(jnp.float32))
    expert_range = (jnp.arange(wave, dtype=jnp.int32) + me) % wave
    hit = expert_ids[:, :, None] == expert_range[None, None, :]
    coef = jnp.sum(jnp.where(hit, gate_probs[:, :, None], 0.0), axis=1)
    member = jnp.any(hit, axis=1).astype(jnp.int32)
    rank = jnp.cumsum(member, axis=0) - 1
    slot_range = jnp.arange(CAP, dtype=jnp.int32)
    picked = (member[:, :, None] == 1) & (rank[:, :, None] == slot_range[None, None, :])
    factor = coef * loss_scale[:, None]
    slot_factor = jnp.sum(jnp.where(picked, factor[:, :, None], 0.0), axis=0).reshape(wave * CAP, 1)
    select = picked.astype(jnp.bfloat16).reshape(-1, wave * CAP)
    chosen_grad = lax.dot_general(select, grad_out, over_rows, preferred_element_type=jnp.float32)
    send_grad = (slot_factor * chosen_grad).astype(jnp.bfloat16)
    send_in = lax.dot_general(
        select, layer_in, over_rows, preferred_element_type=jnp.float32
    ).astype(jnp.bfloat16)
    mine = jnp.concatenate([send_grad[:CAP], send_in[:CAP]])
    other = jnp.concatenate([send_grad[CAP:], send_in[CAP:]])

    swap = [(0, 1), (1, 0)]
    ahead, behind = ring_orders(local_count)
    go = lambda x: lax.ppermute(x, "local", ahead)
    back = lambda x: lax.ppermute(x, "local", behind)
    half = local_count // 2

    near = mine
    far = lax.ppermute(other, "node", swap)

    rows = {0: (near, far)}
    a_f, a_b, b_f, b_b = near, near, far, far
    for s in range(1, half + 1):
        a_f = go(a_f)
        b_b = back(b_b)
        if s < half:
            b_f = go(b_f)
            a_b = back(a_b)
            rows[-s] = (a_f, b_f)
            rows[s] = (a_b, b_b)
        else:
            rows[s] = (a_f, b_b)

    hid = {}
    pieces = {}
    for s, (a, b) in rows.items():
        grads = jnp.concatenate([a[:CAP], b[:CAP]])
        ins = jnp.concatenate([a[CAP:], b[CAP:]])
        gate_pre = lax.dot_general(ins, w_gate, contract, preferred_element_type=jnp.float32)
        up_pre = lax.dot_general(ins, w_up, contract, preferred_element_type=jnp.float32)
        d_act = lax.dot_general(grads, w_down, contract, preferred_element_type=jnp.float32)
        act, slope = silu_parts(gate_pre)
        hidden = (act * up_pre).astype(jnp.bfloat16)
        d_up = (d_act * act).astype(jnp.bfloat16)
        d_gate = (d_act * up_pre * slope).astype(jnp.bfloat16)
        hid[s] = (hidden, d_up, d_gate, grads, ins)
        p = jnp.dot(d_gate, w_gate, preferred_element_type=jnp.float32)
        pieces[s] = p + jnp.dot(d_up, w_up, preferred_element_type=jnp.float32)

    def piece(s, which):
        return pieces[s][which * CAP : (which + 1) * CAP]

    def summed(which, step, far_side, hops):
        carry = None
        for s in range(hops, 0, -1):
            p = piece(s if s == half else far_side * s, which)
            carry = (p if carry is None else p + carry.astype(jnp.float32)).astype(jnp.bfloat16)
            carry = step(carry)
        return carry.astype(jnp.float32)

    total_b = piece(0, 1) + summed(1, back, -1, half) + summed(1, go, 1, half - 1)
    total_a = piece(0, 0) + summed(0, back, -1, half - 1) + summed(0, go, 1, half)
    returned = lax.ppermute(total_b.astype(jnp.bfloat16), "node", swap)
    back_rows = jnp.concatenate([total_a.astype(jnp.bfloat16), returned])
    grad_in = jnp.dot(select, back_rows, preferred_element_type=jnp.float32).astype(jnp.bfloat16)

    hidden, d_up, d_gate, rows_grad, rows_in = (jnp.concatenate(x) for x in zip(*hid.values()))
    grad_down = lax.dot_general(
        hidden, rows_grad, over_rows, preferred_element_type=jnp.float32
    ).astype(jnp.bfloat16)
    grad_gate = lax.dot_general(
        d_gate, rows_in, over_rows, preferred_element_type=jnp.float32
    ).astype(jnp.bfloat16)
    grad_up = lax.dot_general(d_up, rows_in, over_rows, preferred_element_type=jnp.float32).astype(
        jnp.bfloat16
    )
    return (grad_in, grad_gate, grad_up, grad_down)


def solution(mesh):
    nodes, locals_ = mesh.shape["node"], mesh.shape["local"]
    ring = nodes == 2 and locals_ % 2 == 0 and locals_ >= 4

    def per_device(*args):
        shards = FF // args[5].shape[0]
        if ring and shards == locals_:
            return per_device_ring(*args)
        return per_device_exchange(*args)

    return jax.shard_map(
        per_device,
        mesh=mesh,
        in_specs=(
            P(("groups", "node", "local"), None),
            P(("groups", "node", "local"), None),
            P(("groups", "node", "local"), None),
            P(("groups", "node", "local"), None),
            P(("groups", "node", "local"), None),
            P(("node", "local"), None),
            P(("node", "local"), None),
            P(("node", "local"), None),
        ),
        out_specs=(
            P(("groups", "node", "local"), None),
            P(("groups", "node", "local"), None),
            P(("groups", "node", "local"), None),
            P(("groups", "node", "local"), None),
        ),
        check_vma=False,
    )
```

```python
import functools

import jax
import jax.numpy as jnp
from jax import lax
from jax.experimental import pallas as pl
from jax.experimental.pallas import tpu as pltpu
from jax.sharding import PartitionSpec as P

FF = 1536
SAMPLES = 8
TOK_DEV = 128
CAP = 16
BF = jnp.bfloat16
F32 = jnp.float32
NT = (((1,), (1,)), ((), ()))
TN = (((0,), (0,)), ((), ()))
NN = (((1,), (0,)), ((), ()))
IN_VMEM = pl.BlockSpec(memory_space=pltpu.VMEM)
LIGHT = pl.CostEstimate(flops=0, bytes_accessed=0, transcendentals=0)


def silu_parts(pre):
    sigma = jax.nn.sigmoid(pre)
    return (pre * sigma, sigma * (1.0 + pre * (1.0 - sigma)))


def per_device_exchange(grad_out, layer_in, expert_ids, gate_probs, sample_ids, w_gate, w_up, w_down):
    tok_count = grad_out.shape[0]
    width = grad_out.shape[1]
    shard_width = w_gate.shape[0]
    node_count = lax.axis_size("node")
    local_count = lax.axis_size("local")
    devices = node_count * local_count
    shards = FF // shard_width
    wave = devices // shards
    contract = (((1,), (1,)), ((), ()))
    over_rows = (((0,), (0,)), ((), ()))
    packed = sample_ids[0]
    same_sample = packed[:, None] == packed[None, :]
    length = jnp.sum(same_sample.astype(jnp.int32), axis=1)
    loss_scale = TOK_DEV / (SAMPLES * length.astype(jnp.float32))
    expert_range = jnp.arange(wave, dtype=jnp.int32)
    hit = expert_ids[:, :, None] == expert_range[None, None, :]
    coef = jnp.sum(jnp.where(hit, gate_probs[:, :, None], 0.0), axis=1)
    member = jnp.any(hit, axis=1).astype(jnp.int32)
    rank = jnp.cumsum(member, axis=0) - 1
    slot_range = jnp.arange(CAP, dtype=jnp.int32)
    picked = (member[:, :, None] == 1) & (rank[:, :, None] == slot_range[None, None, :])
    factor = coef * loss_scale[:, None]
    slot_factor = jnp.sum(jnp.where(picked, factor[:, :, None], 0.0), axis=0).reshape(wave * CAP, 1)
    select = picked.astype(jnp.bfloat16).reshape(tok_count, wave * CAP)
    chosen_grad = lax.dot_general(select, grad_out, over_rows, preferred_element_type=jnp.float32)
    send_grad = (slot_factor * chosen_grad).astype(jnp.bfloat16)
    send_in = lax.dot_general(
        select, layer_in, over_rows, preferred_element_type=jnp.float32
    ).astype(jnp.bfloat16)
    flat_grad = jnp.broadcast_to(
        send_grad.reshape(wave, 1, CAP, width), (wave, shards, CAP, width)
    ).reshape(devices, CAP, width)
    flat_in = jnp.broadcast_to(
        send_in.reshape(wave, 1, CAP, width), (wave, shards, CAP, width)
    ).reshape(devices, CAP, width)
    recv_grad, recv_in = (
        lax.all_to_all(flat_grad, ("node", "local"), split_axis=0, concat_axis=0, tiled=True),
        lax.all_to_all(flat_in, ("node", "local"), split_axis=0, concat_axis=0, tiled=True),
    )
    rows_grad = recv_grad.reshape(devices * CAP, width)
    rows_in = recv_in.reshape(devices * CAP, width)
    gate_pre = lax.dot_general(rows_in, w_gate, contract, preferred_element_type=jnp.float32)
    up_pre = lax.dot_general(rows_in, w_up, contract, preferred_element_type=jnp.float32)
    d_act = lax.dot_general(rows_grad, w_down, contract, preferred_element_type=jnp.float32)
    act, slope = silu_parts(gate_pre)
    hidden = (act * up_pre).astype(jnp.bfloat16)
    d_up = (d_act * act).astype(jnp.bfloat16)
    d_gate = (d_act * up_pre * slope).astype(jnp.bfloat16)
    grad_down = lax.dot_general(
        hidden, rows_grad, over_rows, preferred_element_type=jnp.float32
    ).astype(jnp.bfloat16)
    grad_gate = lax.dot_general(
        d_gate, rows_in, over_rows, preferred_element_type=jnp.float32
    ).astype(jnp.bfloat16)
    grad_up = lax.dot_general(d_up, rows_in, over_rows, preferred_element_type=jnp.float32).astype(
        jnp.bfloat16
    )
    pieces = jnp.dot(d_gate, w_gate, preferred_element_type=jnp.float32)
    pieces = (pieces + jnp.dot(d_up, w_up, preferred_element_type=jnp.float32)).astype(jnp.bfloat16)
    returned = lax.all_to_all(
        pieces.reshape(devices, CAP, width),
        ("node", "local"),
        split_axis=0,
        concat_axis=0,
        tiled=True,
    )
    returned = returned.reshape(devices * CAP, width)
    select_all = jnp.broadcast_to(
        select.reshape(tok_count, wave, 1, CAP), (tok_count, wave, shards, CAP)
    )
    select_all = select_all.reshape(tok_count, devices * CAP)
    grad_in = jnp.dot(select_all, returned, preferred_element_type=jnp.float32).astype(jnp.bfloat16)
    return (grad_in, grad_gate, grad_up, grad_down)


def ring_orders(count):
    order = list(range(0, count, 2)) + list(range(count - 1, 0, -2))
    ahead = [(order[i], order[(i + 1) % count]) for i in range(count)]
    behind = [(order[i], order[(i - 1) % count]) for i in range(count)]
    return ahead, behind


def dot(x, y, dims=NN):
    return lax.dot_general(x, y, dims, preferred_element_type=F32)


def held(x):
    return pltpu.with_memory_space_constraint(x, pltpu.VMEM)


def streamed(x):
    return pltpu.with_memory_space_constraint(x, pltpu.HBM)


def after(x, *earlier):
    return lax.optimization_barrier((x, *earlier))[0]


def together(*arrays):
    return lax.optimization_barrier(arrays)


def in_vmem(*shape, dtype=BF):
    return pltpu.MemorySpace.VMEM(shape, dtype)


def tiles_of(width, tile):
    return [pl.ds(k, min(tile, width - k)) for k in range(0, width, tile)]


def pick_kernel(ids_hbm, probs_hbm, samples_hbm, grad_hbm, in_hbm, mine_ref, other_ref, select_ref, *scratch):
    ids_ref, probs_ref, samples_ref, grad_ref, in_ref, sem = scratch
    sources = (ids_hbm, probs_hbm, samples_hbm, grad_hbm, in_hbm)
    copies = [pltpu.make_async_copy(x, y, sem.at[i]) for i, (x, y) in enumerate(zip(sources, scratch))]
    for copy in copies:
        copy.start()
    count = grad_ref.shape[0]
    me = lax.axis_index("node")
    upto = lax.broadcasted_iota(jnp.int32, (count, count), 0) <= lax.broadcasted_iota(
        jnp.int32, (count, count), 1
    )
    upto = upto.astype(F32).astype(BF)
    slot = lax.broadcasted_iota(jnp.int32, (CAP, count), 0).astype(F32) + 1.0
    for copy in copies[:3]:
        copy.wait()
    ids, probs = ids_ref[...], probs_ref[...]
    sample = jnp.broadcast_to(samples_ref[...].astype(F32), (count, count))
    length = jnp.sum((sample == sample.T).astype(F32), axis=0, keepdims=True)
    loss_scale = TOK_DEV / (SAMPLES * length)
    selects, factors = [], []
    for i in range(2):
        hit = ids == (me + i) % 2
        coef = jnp.sum(jnp.where(hit, probs, 0.0), axis=0, keepdims=True)
        member = jnp.max(hit.astype(F32), axis=0, keepdims=True)
        rank = dot(jnp.broadcast_to(member, (CAP, count)).astype(BF), upto)
        picked = (rank == slot) & (member > 0.0)
        selects.append(picked.astype(F32))
        factors.append(jnp.sum(jnp.where(picked, coef * loss_scale, 0.0), axis=1, keepdims=True))
    select = jnp.concatenate(selects).astype(BF)
    factor = jnp.concatenate(factors)
    select_ref[...] = select
    tiles = tiles_of(grad_ref.shape[1], 1024)
    copies[3].wait()
    for k in tiles:
        grads = (factor * dot(select, grad_ref[:, k])).astype(BF)
        mine_ref[:CAP, k] = grads[:CAP]
        other_ref[:CAP, k] = grads[CAP:]
    copies[4].wait()
    for k in tiles:
        ins = dot(select, in_ref[:, k]).astype(BF)
        mine_ref[CAP:, k] = ins[:CAP]
        other_ref[CAP:, k] = ins[CAP:]


def pick(*arrays):
    count, width = arrays[-1].shape
    return pl.pallas_call(
        pick_kernel,
        in_specs=[pl.BlockSpec(memory_space=pltpu.HBM)] * 5,
        out_specs=[IN_VMEM] * 3,
        out_shape=[in_vmem(2 * CAP, width), in_vmem(2 * CAP, width), in_vmem(2 * CAP, count)],
        scratch_shapes=[pltpu.VMEM(x.shape, x.dtype) for x in arrays] + [pltpu.SemaphoreType.DMA((5,))],
        compiler_params=pltpu.CompilerParams(vmem_limit_bytes=8 << 20),
        name="pick",
    )(*[streamed(x) for x in arrays])


def load_kernel(n, *refs):
    copies = [pltpu.make_async_copy(refs[i], refs[n + i], refs[2 * n].at[i]) for i in range(n)]
    for copy in copies:
        copy.start()
    for copy in copies:
        copy.wait()


def load(*arrays):
    n = len(arrays)
    return pl.pallas_call(
        functools.partial(load_kernel, n),
        in_specs=[pl.BlockSpec(memory_space=pltpu.HBM)] * n,
        out_specs=[IN_VMEM] * n,
        out_shape=[in_vmem(*x.shape) for x in arrays],
        scratch_shapes=[pltpu.SemaphoreType.DMA((n,))],
        cost_estimate=LIGHT,
        compiler_params=pltpu.CompilerParams(vmem_limit_bytes=1 << 20),
        name="load",
    )(*[streamed(x) for x in arrays])


def work_kernel(n, *refs):
    blocks, (gate_ref, up_ref, down_ref) = refs[:n], refs[n : n + 3]
    pieces = refs[n + 3 : 2 * n + 3]
    hidden_ref, d_up_ref, d_gate_ref, grads_ref, ins_ref = refs[2 * n + 3 :]
    for i, block in enumerate(blocks):
        rows = pl.ds(i * CAP, CAP)
        grads_ref[rows, :] = block[:CAP, :]
        ins_ref[rows, :] = block[CAP:, :]
    gate_pre = jnp.zeros((n * CAP, gate_ref.shape[0]), F32)
    up_pre = d_act = gate_pre
    for k in tiles_of(gate_ref.shape[1], 1024):
        gate_pre += dot(ins_ref[:, k], gate_ref[:, k], NT)
        up_pre += dot(ins_ref[:, k], up_ref[:, k], NT)
        d_act += dot(grads_ref[:, k], down_ref[:, k], NT)
    act, slope = silu_parts(gate_pre)
    d_up = (d_act * act).astype(BF)
    d_gate = (d_act * up_pre * slope).astype(BF)
    hidden_ref[...] = (act * up_pre).astype(BF)
    d_up_ref[...] = d_up
    d_gate_ref[...] = d_gate
    for k in tiles_of(gate_ref.shape[1], 1024):
        p = (dot(d_gate, gate_ref[:, k]) + dot(d_up, up_ref[:, k])).astype(BF)
        for i, piece in enumerate(pieces):
            piece[:, k] = p[i * CAP : (i + 1) * CAP]


def work(blocks, w_gate, w_up, w_down):
    n = len(blocks)
    hid, width = w_gate.shape
    outs = [in_vmem(CAP, width)] * n + [in_vmem(n * CAP, hid)] * 3 + [in_vmem(n * CAP, width)] * 2
    out = pl.pallas_call(
        functools.partial(work_kernel, n),
        in_specs=[IN_VMEM] * (n + 3),
        out_specs=[IN_VMEM] * len(outs),
        out_shape=outs,
        cost_estimate=LIGHT,
        compiler_params=pltpu.CompilerParams(vmem_limit_bytes=4 << 20),
        name="work",
    )(*[held(x) for x in blocks], held(w_gate), held(w_up), held(w_down))
    return out[:n], out[n:]


def weight_grads_kernel(n, *refs):
    hidden, d_up, d_gate, grads, ins = (refs[i * n : (i + 1) * n] for i in range(5))
    outs, (buffer, sem) = refs[5 * n : 5 * n + 3], refs[5 * n + 3 :]
    copies = []
    for i, (left, right) in enumerate(((d_gate, ins), (d_up, ins), (hidden, grads))):
        across = jnp.concatenate([x[...] for x in left]).astype(F32).T.astype(BF)
        for k in tiles_of(buffer.shape[2], 512):
            buffer[i, :, k] = dot(across, jnp.concatenate([x[:, k] for x in right])).astype(BF)
        copies.append(pltpu.make_async_copy(buffer.at[i], outs[i], sem.at[i]))
        copies[i].start()
    for copy in copies:
        copy.wait()


def weight_grads(saved):
    n = len(saved)
    hid, width = saved[0][0].shape[1], saved[0][3].shape[1]
    return pl.pallas_call(
        functools.partial(weight_grads_kernel, n),
        in_specs=[IN_VMEM] * (5 * n),
        out_specs=[pl.BlockSpec(memory_space=pl.ANY)] * 3,
        out_shape=[jax.ShapeDtypeStruct((hid, width), BF)] * 3,
        scratch_shapes=[pltpu.VMEM((3, hid, width), BF), pltpu.SemaphoreType.DMA((3,))],
        cost_estimate=LIGHT,
        compiler_params=pltpu.CompilerParams(vmem_limit_bytes=8 << 20),
        name="weight_grads",
    )(*[held(x) for part in zip(*saved) for x in part])


def place_kernel(select_ref, own_ref, ahead_ref, behind_ref, first_ref, second_ref, out_ref, rows_ref, buffer, sem):
    spread = select_ref[...].astype(F32).T.astype(BF)
    for k in tiles_of(out_ref.shape[1], 1024):
        here = own_ref[:, k].astype(F32) + ahead_ref[:, k].astype(F32) + behind_ref[:, k].astype(F32)
        there = first_ref[:, k].astype(F32) + second_ref[:, k].astype(F32)
        rows_ref[:CAP, k] = here.astype(BF)
        rows_ref[CAP:, k] = there.astype(BF)
    copies = []
    for j, r in enumerate(tiles_of(out_ref.shape[0], buffer.shape[0] // 2)):
        for k in tiles_of(out_ref.shape[1], 1024):
            buffer[r, k] = dot(spread[r.start : r.start + r.size], rows_ref[:, k]).astype(BF)
        copies.append(pltpu.make_async_copy(buffer.at[r], out_ref.at[r], sem.at[j]))
        copies[j].start()
    for copy in copies:
        copy.wait()


def place(select, own, ahead, behind, first, second):
    count, width = select.shape[1], own.shape[1]
    return pl.pallas_call(
        place_kernel,
        in_specs=[IN_VMEM] * 6,
        out_specs=pl.BlockSpec(memory_space=pl.ANY),
        out_shape=jax.ShapeDtypeStruct((count, width), BF),
        scratch_shapes=[pltpu.VMEM((2 * CAP, width), BF), pltpu.VMEM((count, width), BF), pltpu.SemaphoreType.DMA((2,))],
        compiler_params=pltpu.CompilerParams(vmem_limit_bytes=8 << 20),
        name="place",
    )(*[held(x) for x in (select, own, ahead, behind, first, second)])


def per_device_ring(grad_out, layer_in, expert_ids, gate_probs, sample_ids, w_gate, w_up, w_down):
    swap = [(0, 1), (1, 0)]
    ahead, behind = ring_orders(lax.axis_size("local"))
    half = lax.axis_size("local") // 2

    def go(x):
        return lax.ppermute(x, "local", ahead)

    def back(x):
        return lax.ppermute(x, "local", behind)

    near, other, select = pick(expert_ids.T, gate_probs.T, sample_ids, grad_out, layer_in)
    far = lax.ppermute(other, "node", swap)

    weights = load(w_gate, w_up, w_down)
    saved = []
    pieces = {}

    def work_on(members):
        outs, keep = work([rows[member] for member in members], *weights)
        pieces.update(zip(members, outs))
        saved.append(keep)
        return keep[0]

    rows = {(0, 0): near, (0, 1): far}
    near_go, near_back, far_go, far_back = near, near, far, far
    for s in range(1, half):
        near_go, near_back = go(near_go), back(near_back)
        if s == 2:
            far_go, far_back = after(far_go, weights[0]), after(far_back, weights[0])
        far_go, far_back = go(far_go), back(far_back)
        rows.update({(-s, 0): near_go, (s, 0): near_back, (-s, 1): far_go, (s, 1): far_back})
        if s == half - 2:
            done = work_on(list(rows)[:-2])
            near_go, near_back = after(near_go, done), after(near_back, done)
    near_go, near_back = together(near_go, near_back)
    far_go, far_back = together(far_go, far_back)
    near_go = go(near_go)
    far_back = back(far_back)
    rows.update({(half, 0): near_go, (half, 1): far_back})
    work_on([member for member in rows if member not in pieces])

    def add(x, y):
        return (x.astype(F32) + y.astype(F32)).astype(BF)

    far_long, near_long = pieces[half, 1], pieces[half, 0]
    far_short, near_short = pieces[half - 1, 1], pieces[1 - half, 0]
    for s in range(half - 1, 0, -1):
        far_long, near_long = back(far_long), go(near_long)
        far_short, near_short = go(far_short), back(near_short)
        far_long, near_long = add(pieces[-s, 1], far_long), add(pieces[s, 0], near_long)
        if s > 1:
            far_short, near_short = add(pieces[s - 1, 1], far_short), add(pieces[1 - s, 0], near_short)
            far_short, near_short = after(far_short, far_long), after(near_short, near_long)
    saved[0] = [after(saved[0][0], far_long, near_long), *saved[0][1:]]
    grad_gate, grad_up, grad_down = weight_grads(saved)
    far_long, near_long = back(far_long), go(near_long)
    first = lax.ppermute(after(add(pieces[0, 1], far_short), grad_gate), "node", swap)
    second = lax.ppermute(far_long, "node", swap)
    grad_in = place(select, pieces[0, 0], near_long, near_short, first, second)
    return (grad_in, grad_gate, grad_up, grad_down)


def solution(mesh):
    nodes, locals_ = mesh.shape["node"], mesh.shape["local"]
    ring = nodes == 2 and locals_ % 2 == 0 and locals_ >= 8

    def per_device(*args):
        shards = FF // args[5].shape[0]
        if ring and shards == locals_:
            return per_device_ring(*args)
        return per_device_exchange(*args)

    return jax.shard_map(
        per_device,
        mesh=mesh,
        in_specs=(
            P(("groups", "node", "local"), None),
            P(("groups", "node", "local"), None),
            P(("groups", "node", "local"), None),
            P(("groups", "node", "local"), None),
            P(("groups", "node", "local"), None),
            P(("node", "local"), None),
            P(("node", "local"), None),
            P(("node", "local"), None),
        ),
        out_specs=(
            P(("groups", "node", "local"), None),
            P(("groups", "node", "local"), None),
            P(("groups", "node", "local"), None),
            P(("groups", "node", "local"), None),
        ),
        check_vma=False,
    )
```

```python
import functools

import jax
import jax.numpy as jnp
from jax import lax
from jax.experimental import pallas as pl
from jax.experimental.pallas import tpu as pltpu
from jax.sharding import PartitionSpec as P

FF = 1536
SAMPLES = 8
TOK_DEV = 128
CAP = 16
BF = jnp.bfloat16
WORK_COST = pl.CostEstimate(flops=3000000000, bytes_accessed=0, transcendentals=0)
F32 = jnp.float32
NT = (((1,), (1,)), ((), ()))
TN = (((0,), (0,)), ((), ()))
NN = (((1,), (0,)), ((), ()))
IN_VMEM = pl.BlockSpec(memory_space=pltpu.VMEM)
LIGHT = pl.CostEstimate(flops=0, bytes_accessed=0, transcendentals=0)


def silu_parts(pre):
    sigma = jax.nn.sigmoid(pre)
    return (pre * sigma, sigma * (1.0 + pre * (1.0 - sigma)))


def per_device_exchange(grad_out, layer_in, expert_ids, gate_probs, sample_ids, w_gate, w_up, w_down):
    tok_count = grad_out.shape[0]
    width = grad_out.shape[1]
    shard_width = w_gate.shape[0]
    node_count = lax.axis_size("node")
    local_count = lax.axis_size("local")
    devices = node_count * local_count
    shards = FF // shard_width
    wave = devices // shards
    contract = (((1,), (1,)), ((), ()))
    over_rows = (((0,), (0,)), ((), ()))
    packed = sample_ids[0]
    same_sample = packed[:, None] == packed[None, :]
    length = jnp.sum(same_sample.astype(jnp.int32), axis=1)
    loss_scale = TOK_DEV / (SAMPLES * length.astype(jnp.float32))
    expert_range = jnp.arange(wave, dtype=jnp.int32)
    hit = expert_ids[:, :, None] == expert_range[None, None, :]
    coef = jnp.sum(jnp.where(hit, gate_probs[:, :, None], 0.0), axis=1)
    member = jnp.any(hit, axis=1).astype(jnp.int32)
    rank = jnp.cumsum(member, axis=0) - 1
    slot_range = jnp.arange(CAP, dtype=jnp.int32)
    picked = (member[:, :, None] == 1) & (rank[:, :, None] == slot_range[None, None, :])
    factor = coef * loss_scale[:, None]
    slot_factor = jnp.sum(jnp.where(picked, factor[:, :, None], 0.0), axis=0).reshape(wave * CAP, 1)
    select = picked.astype(jnp.bfloat16).reshape(tok_count, wave * CAP)
    chosen_grad = lax.dot_general(select, grad_out, over_rows, preferred_element_type=jnp.float32)
    send_grad = (slot_factor * chosen_grad).astype(jnp.bfloat16)
    send_in = lax.dot_general(
        select, layer_in, over_rows, preferred_element_type=jnp.float32
    ).astype(jnp.bfloat16)
    flat_grad = jnp.broadcast_to(
        send_grad.reshape(wave, 1, CAP, width), (wave, shards, CAP, width)
    ).reshape(devices, CAP, width)
    flat_in = jnp.broadcast_to(
        send_in.reshape(wave, 1, CAP, width), (wave, shards, CAP, width)
    ).reshape(devices, CAP, width)
    recv_grad, recv_in = (
        lax.all_to_all(flat_grad, ("node", "local"), split_axis=0, concat_axis=0, tiled=True),
        lax.all_to_all(flat_in, ("node", "local"), split_axis=0, concat_axis=0, tiled=True),
    )
    rows_grad = recv_grad.reshape(devices * CAP, width)
    rows_in = recv_in.reshape(devices * CAP, width)
    gate_pre = lax.dot_general(rows_in, w_gate, contract, preferred_element_type=jnp.float32)
    up_pre = lax.dot_general(rows_in, w_up, contract, preferred_element_type=jnp.float32)
    d_act = lax.dot_general(rows_grad, w_down, contract, preferred_element_type=jnp.float32)
    act, slope = silu_parts(gate_pre)
    hidden = (act * up_pre).astype(jnp.bfloat16)
    d_up = (d_act * act).astype(jnp.bfloat16)
    d_gate = (d_act * up_pre * slope).astype(jnp.bfloat16)
    grad_down = lax.dot_general(
        hidden, rows_grad, over_rows, preferred_element_type=jnp.float32
    ).astype(jnp.bfloat16)
    grad_gate = lax.dot_general(
        d_gate, rows_in, over_rows, preferred_element_type=jnp.float32
    ).astype(jnp.bfloat16)
    grad_up = lax.dot_general(d_up, rows_in, over_rows, preferred_element_type=jnp.float32).astype(
        jnp.bfloat16
    )
    pieces = jnp.dot(d_gate, w_gate, preferred_element_type=jnp.float32)
    pieces = (pieces + jnp.dot(d_up, w_up, preferred_element_type=jnp.float32)).astype(jnp.bfloat16)
    returned = lax.all_to_all(
        pieces.reshape(devices, CAP, width),
        ("node", "local"),
        split_axis=0,
        concat_axis=0,
        tiled=True,
    )
    returned = returned.reshape(devices * CAP, width)
    select_all = jnp.broadcast_to(
        select.reshape(tok_count, wave, 1, CAP), (tok_count, wave, shards, CAP)
    )
    select_all = select_all.reshape(tok_count, devices * CAP)
    grad_in = jnp.dot(select_all, returned, preferred_element_type=jnp.float32).astype(jnp.bfloat16)
    return (grad_in, grad_gate, grad_up, grad_down)


def ring_orders(count):
    order = list(range(0, count, 2)) + list(range(count - 1, 0, -2))
    ahead = [(order[i], order[(i + 1) % count]) for i in range(count)]
    behind = [(order[i], order[(i - 1) % count]) for i in range(count)]
    return ahead, behind


def dot(x, y, dims=NN):
    return lax.dot_general(x, y, dims, preferred_element_type=F32)


def held(x):
    return pltpu.with_memory_space_constraint(x, pltpu.VMEM)


def streamed(x):
    return pltpu.with_memory_space_constraint(x, pltpu.HBM)


def after(x, *earlier):
    return lax.optimization_barrier((x, *earlier))[0]


def together(*arrays):
    return lax.optimization_barrier(arrays)


def in_vmem(*shape, dtype=BF):
    return pltpu.MemorySpace.VMEM(shape, dtype)


def tiles_of(width, tile):
    return [pl.ds(k, min(tile, width - k)) for k in range(0, width, tile)]


def pick_kernel(ids_hbm, probs_hbm, samples_hbm, grad_hbm, in_hbm, mine_ref, other_ref, select_ref, *scratch):
    ids_ref, probs_ref, samples_ref, grad_ref, in_ref, sem = scratch
    sources = (ids_hbm, probs_hbm, samples_hbm, grad_hbm, in_hbm)
    copies = [pltpu.make_async_copy(x, y, sem.at[i]) for i, (x, y) in enumerate(zip(sources, scratch))]
    for copy in copies:
        copy.start()
    count = grad_ref.shape[0]
    me = lax.axis_index("node")
    upto = lax.broadcasted_iota(jnp.int32, (count, count), 0) <= lax.broadcasted_iota(
        jnp.int32, (count, count), 1
    )
    upto = upto.astype(F32).astype(BF)
    slot = lax.broadcasted_iota(jnp.int32, (CAP, count), 0).astype(F32) + 1.0
    for copy in copies[:3]:
        copy.wait()
    ids, probs = ids_ref[...], probs_ref[...]
    sample = jnp.broadcast_to(samples_ref[...].astype(F32), (count, count))
    length = jnp.sum((sample == sample.T).astype(F32), axis=0, keepdims=True)
    loss_scale = TOK_DEV / (SAMPLES * length)
    selects, factors = [], []
    for i in range(2):
        hit = ids == (me + i) % 2
        coef = jnp.sum(jnp.where(hit, probs, 0.0), axis=0, keepdims=True)
        member = jnp.max(hit.astype(F32), axis=0, keepdims=True)
        rank = dot(jnp.broadcast_to(member, (CAP, count)).astype(BF), upto)
        picked = (rank == slot) & (member > 0.0)
        selects.append(picked.astype(F32))
        factors.append(jnp.sum(jnp.where(picked, coef * loss_scale, 0.0), axis=1, keepdims=True))
    select = jnp.concatenate(selects).astype(BF)
    factor = jnp.concatenate(factors)
    select_ref[...] = select
    tiles = tiles_of(grad_ref.shape[1], 1024)
    copies[3].wait()
    for k in tiles:
        grads = (factor * dot(select, grad_ref[:, k])).astype(BF)
        mine_ref[:CAP, k] = grads[:CAP]
        other_ref[:CAP, k] = grads[CAP:]
    copies[4].wait()
    for k in tiles:
        ins = dot(select, in_ref[:, k]).astype(BF)
        mine_ref[CAP:, k] = ins[:CAP]
        other_ref[CAP:, k] = ins[CAP:]


def pick(*arrays):
    count, width = arrays[-1].shape
    return pl.pallas_call(
        pick_kernel,
        in_specs=[pl.BlockSpec(memory_space=pltpu.HBM)] * 5,
        out_specs=[IN_VMEM] * 3,
        out_shape=[in_vmem(2 * CAP, width), in_vmem(2 * CAP, width), in_vmem(2 * CAP, count)],
        scratch_shapes=[pltpu.VMEM(x.shape, x.dtype) for x in arrays] + [pltpu.SemaphoreType.DMA((5,))],
        compiler_params=pltpu.CompilerParams(vmem_limit_bytes=8 << 20),
        name="pick",
    )(*[streamed(x) for x in arrays])


def load_kernel(n, *refs):
    copies = [pltpu.make_async_copy(refs[i], refs[n + i], refs[2 * n].at[i]) for i in range(n)]
    for copy in copies:
        copy.start()
    for copy in copies:
        copy.wait()


def load(*arrays):
    n = len(arrays)
    return pl.pallas_call(
        functools.partial(load_kernel, n),
        in_specs=[pl.BlockSpec(memory_space=pltpu.HBM)] * n,
        out_specs=[IN_VMEM] * n,
        out_shape=[in_vmem(*x.shape) for x in arrays],
        scratch_shapes=[pltpu.SemaphoreType.DMA((n,))],
        cost_estimate=LIGHT,
        compiler_params=pltpu.CompilerParams(vmem_limit_bytes=1 << 20),
        name="load",
    )(*[streamed(x) for x in arrays])


def work_kernel(n, *refs):
    blocks, (gate_ref, up_ref, down_ref) = refs[:n], refs[n : n + 3]
    pieces = refs[n + 3 : 2 * n + 3]
    hidden_ref, d_up_ref, d_gate_ref, grads_ref, ins_ref = refs[2 * n + 3 :]
    for i, block in enumerate(blocks):
        rows = pl.ds(i * CAP, CAP)
        grads_ref[rows, :] = block[:CAP, :]
        ins_ref[rows, :] = block[CAP:, :]
    gate_pre = jnp.zeros((n * CAP, gate_ref.shape[0]), F32)
    up_pre = d_act = gate_pre
    for k in tiles_of(gate_ref.shape[1], 1024):
        gate_pre += dot(ins_ref[:, k], gate_ref[:, k], NT)
        up_pre += dot(ins_ref[:, k], up_ref[:, k], NT)
        d_act += dot(grads_ref[:, k], down_ref[:, k], NT)
    act, slope = silu_parts(gate_pre)
    d_up = (d_act * act).astype(BF)
    d_gate = (d_act * up_pre * slope).astype(BF)
    hidden_ref[...] = (act * up_pre).astype(BF)
    d_up_ref[...] = d_up
    d_gate_ref[...] = d_gate
    for k in tiles_of(gate_ref.shape[1], 1024):
        p = (dot(d_gate, gate_ref[:, k]) + dot(d_up, up_ref[:, k])).astype(BF)
        for i, piece in enumerate(pieces):
            piece[:, k] = p[i * CAP : (i + 1) * CAP]


def work(blocks, w_gate, w_up, w_down, flops):
    n = len(blocks)
    hid, width = w_gate.shape
    outs = [in_vmem(CAP, width)] * n + [in_vmem(n * CAP, hid)] * 3 + [in_vmem(n * CAP, width)] * 2
    out = pl.pallas_call(
        functools.partial(work_kernel, n),
        in_specs=[IN_VMEM] * (n + 3),
        out_specs=[IN_VMEM] * len(outs),
        out_shape=outs,
        cost_estimate=pl.CostEstimate(flops=flops, bytes_accessed=0, transcendentals=0),
        compiler_params=pltpu.CompilerParams(vmem_limit_bytes=4 << 20),
        name="work",
    )(*[held(x) for x in blocks], held(w_gate), held(w_up), held(w_down))
    return out[:n], out[n:]


def weight_grads_kernel(n, *refs):
    hidden, d_up, d_gate, grads, ins = (refs[i * n : (i + 1) * n] for i in range(5))
    outs, (buffer, sem) = refs[5 * n : 5 * n + 3], refs[5 * n + 3 :]
    copies = []
    for i, (left, right) in enumerate(((d_gate, ins), (d_up, ins), (hidden, grads))):
        across = jnp.concatenate([x[...] for x in left]).astype(F32).T.astype(BF)
        for k in tiles_of(buffer.shape[2], 512):
            buffer[i, :, k] = dot(across, jnp.concatenate([x[:, k] for x in right])).astype(BF)
        copies.append(pltpu.make_async_copy(buffer.at[i], outs[i], sem.at[i]))
        copies[i].start()
    for copy in copies:
        copy.wait()


def weight_grads(saved):
    n = len(saved)
    hid, width = saved[0][0].shape[1], saved[0][3].shape[1]
    return pl.pallas_call(
        functools.partial(weight_grads_kernel, n),
        in_specs=[IN_VMEM] * (5 * n),
        out_specs=[pl.BlockSpec(memory_space=pl.ANY)] * 3,
        out_shape=[jax.ShapeDtypeStruct((hid, width), BF)] * 3,
        scratch_shapes=[pltpu.VMEM((3, hid, width), BF), pltpu.SemaphoreType.DMA((3,))],
        cost_estimate=WORK_COST,
        compiler_params=pltpu.CompilerParams(vmem_limit_bytes=8 << 20),
        name="weight_grads",
    )(*[held(x) for part in zip(*saved) for x in part])


def place_kernel(select_ref, own_ref, ahead_ref, behind_ref, first_ref, second_ref, out_ref, rows_ref, buffer, sem):
    spread = select_ref[...].astype(F32).T.astype(BF)
    for k in tiles_of(out_ref.shape[1], 1024):
        here = own_ref[:, k].astype(F32) + ahead_ref[:, k].astype(F32) + behind_ref[:, k].astype(F32)
        there = first_ref[:, k].astype(F32) + second_ref[:, k].astype(F32)
        rows_ref[:CAP, k] = here.astype(BF)
        rows_ref[CAP:, k] = there.astype(BF)
    copies = []
    for j, r in enumerate(tiles_of(out_ref.shape[0], buffer.shape[0] // 2)):
        for k in tiles_of(out_ref.shape[1], 1024):
            buffer[r, k] = dot(spread[r.start : r.start + r.size], rows_ref[:, k]).astype(BF)
        copies.append(pltpu.make_async_copy(buffer.at[r], out_ref.at[r], sem.at[j]))
        copies[j].start()
    for copy in copies:
        copy.wait()


def place(select, own, ahead, behind, first, second):
    count, width = select.shape[1], own.shape[1]
    return pl.pallas_call(
        place_kernel,
        in_specs=[IN_VMEM] * 6,
        out_specs=pl.BlockSpec(memory_space=pl.ANY),
        out_shape=jax.ShapeDtypeStruct((count, width), BF),
        scratch_shapes=[pltpu.VMEM((2 * CAP, width), BF), pltpu.VMEM((count, width), BF), pltpu.SemaphoreType.DMA((2,))],
        compiler_params=pltpu.CompilerParams(vmem_limit_bytes=8 << 20),
        name="place",
    )(*[held(x) for x in (select, own, ahead, behind, first, second)])


def per_device_ring(grad_out, layer_in, expert_ids, gate_probs, sample_ids, w_gate, w_up, w_down):
    swap = [(0, 1), (1, 0)]
    ahead, behind = ring_orders(lax.axis_size("local"))
    half = lax.axis_size("local") // 2

    def go(x):
        return lax.ppermute(x, "local", ahead)

    def back(x):
        return lax.ppermute(x, "local", behind)

    def cross(x, hops):
        count = lax.axis_size("local")
        pairs = [(i * count + a, (1 - i) * count + b) for i in (0, 1) for a, b in hops]
        return lax.ppermute(x, ("node", "local"), pairs)

    near, other, select = pick(expert_ids.T, gate_probs.T, sample_ids, grad_out, layer_in)
    far = lax.ppermute(other, "node", swap)

    weights = load(w_gate, w_up, w_down)
    saved = []
    pieces = {}

    def work_on(members, flops=0):
        outs, keep = work([rows[member] for member in members], *weights, flops)
        pieces.update(zip(members, outs))
        saved.append(keep)
        return keep[0]

    rows = {(0, 0): near, (0, 1): far}
    near_go, near_back, far_go, far_back = near, near, far, far
    for s in range(1, half):
        near_go, near_back = go(near_go), back(near_back)
        if s == 2:
            far_go, far_back = after(far_go, weights[0]), after(far_back, weights[0])
        far_go, far_back = go(far_go), back(far_back)
        rows.update({(-s, 0): near_go, (s, 0): near_back, (-s, 1): far_go, (s, 1): far_back})
        if s == half - 2:
            done = work_on(list(rows)[:-2], 3000000000)
            far_go, far_back = after(far_go, done), after(far_back, done)
    near_go, near_back = together(near_go, near_back)
    far_go, far_back = together(far_go, far_back)
    near_go = go(near_go)
    far_back = back(far_back)
    rows.update({(half, 0): near_go, (half, 1): far_back})
    work_on([member for member in rows if member not in pieces], 0)

    def add(x, y):
        return (x.astype(F32) + y.astype(F32)).astype(BF)

    far_long, near_long = pieces[half, 1], pieces[half, 0]
    far_short, near_short = pieces[half - 1, 1], pieces[1 - half, 0]
    for s in range(half - 1, 0, -1):
        far_long, near_long = back(far_long), go(near_long)
        far_short, near_short = go(far_short), back(near_short)
        far_long, near_long = add(pieces[-s, 1], far_long), add(pieces[s, 0], near_long)
        if s > 1:
            far_short, near_short = add(pieces[s - 1, 1], far_short), add(pieces[1 - s, 0], near_short)
            far_short, near_short = after(far_short, far_long), after(near_short, near_long)
    saved[0] = [after(saved[0][0], far_long, near_long), *saved[0][1:]]
    grad_gate, grad_up, grad_down = weight_grads(saved)
    far_long, near_long = cross(far_long, behind), go(near_long)
    first = lax.ppermute(add(pieces[0, 1], far_short), "node", swap)
    grad_in = place(select, pieces[0, 0], near_long, near_short, first, far_long)
    return (grad_in, grad_gate, grad_up, grad_down)


def solution(mesh):
    nodes, locals_ = mesh.shape["node"], mesh.shape["local"]
    ring = nodes == 2 and locals_ % 2 == 0 and locals_ >= 8

    def per_device(*args):
        shards = FF // args[5].shape[0]
        if ring and shards == locals_:
            return per_device_ring(*args)
        return per_device_exchange(*args)

    return jax.shard_map(
        per_device,
        mesh=mesh,
        in_specs=(
            P(("groups", "node", "local"), None),
            P(("groups", "node", "local"), None),
            P(("groups", "node", "local"), None),
            P(("groups", "node", "local"), None),
            P(("groups", "node", "local"), None),
            P(("node", "local"), None),
            P(("node", "local"), None),
            P(("node", "local"), None),
        ),
        out_specs=(
            P(("groups", "node", "local"), None),
            P(("groups", "node", "local"), None),
            P(("groups", "node", "local"), None),
            P(("groups", "node", "local"), None),
        ),
        check_vma=False,
    )
```

```python
import functools

import jax
import jax.numpy as jnp
from jax import lax
from jax.experimental import pallas as pl
from jax.experimental.pallas import tpu as pltpu
from jax.sharding import PartitionSpec as P

FF = 1536
SAMPLES = 8
TOK_DEV = 128
CAP = 16
BF = jnp.bfloat16
WORK_COST = pl.CostEstimate(flops=3000000000, bytes_accessed=0, transcendentals=0)
F32 = jnp.float32
NT = (((1,), (1,)), ((), ()))
TN = (((0,), (0,)), ((), ()))
NN = (((1,), (0,)), ((), ()))
IN_VMEM = pl.BlockSpec(memory_space=pltpu.VMEM)
LIGHT = pl.CostEstimate(flops=0, bytes_accessed=0, transcendentals=0)


def silu_parts(pre):
    sigma = jax.nn.sigmoid(pre)
    return (pre * sigma, sigma * (1.0 + pre * (1.0 - sigma)))


def per_device_exchange(grad_out, layer_in, expert_ids, gate_probs, sample_ids, w_gate, w_up, w_down):
    tok_count = grad_out.shape[0]
    width = grad_out.shape[1]
    shard_width = w_gate.shape[0]
    node_count = lax.axis_size("node")
    local_count = lax.axis_size("local")
    devices = node_count * local_count
    shards = FF // shard_width
    wave = devices // shards
    contract = (((1,), (1,)), ((), ()))
    over_rows = (((0,), (0,)), ((), ()))
    packed = sample_ids[0]
    same_sample = packed[:, None] == packed[None, :]
    length = jnp.sum(same_sample.astype(jnp.int32), axis=1)
    loss_scale = TOK_DEV / (SAMPLES * length.astype(jnp.float32))
    expert_range = jnp.arange(wave, dtype=jnp.int32)
    hit = expert_ids[:, :, None] == expert_range[None, None, :]
    coef = jnp.sum(jnp.where(hit, gate_probs[:, :, None], 0.0), axis=1)
    member = jnp.any(hit, axis=1).astype(jnp.int32)
    rank = jnp.cumsum(member, axis=0) - 1
    slot_range = jnp.arange(CAP, dtype=jnp.int32)
    picked = (member[:, :, None] == 1) & (rank[:, :, None] == slot_range[None, None, :])
    factor = coef * loss_scale[:, None]
    slot_factor = jnp.sum(jnp.where(picked, factor[:, :, None], 0.0), axis=0).reshape(wave * CAP, 1)
    select = picked.astype(jnp.bfloat16).reshape(tok_count, wave * CAP)
    chosen_grad = lax.dot_general(select, grad_out, over_rows, preferred_element_type=jnp.float32)
    send_grad = (slot_factor * chosen_grad).astype(jnp.bfloat16)
    send_in = lax.dot_general(
        select, layer_in, over_rows, preferred_element_type=jnp.float32
    ).astype(jnp.bfloat16)
    flat_grad = jnp.broadcast_to(
        send_grad.reshape(wave, 1, CAP, width), (wave, shards, CAP, width)
    ).reshape(devices, CAP, width)
    flat_in = jnp.broadcast_to(
        send_in.reshape(wave, 1, CAP, width), (wave, shards, CAP, width)
    ).reshape(devices, CAP, width)
    recv_grad, recv_in = (
        lax.all_to_all(flat_grad, ("node", "local"), split_axis=0, concat_axis=0, tiled=True),
        lax.all_to_all(flat_in, ("node", "local"), split_axis=0, concat_axis=0, tiled=True),
    )
    rows_grad = recv_grad.reshape(devices * CAP, width)
    rows_in = recv_in.reshape(devices * CAP, width)
    gate_pre = lax.dot_general(rows_in, w_gate, contract, preferred_element_type=jnp.float32)
    up_pre = lax.dot_general(rows_in, w_up, contract, preferred_element_type=jnp.float32)
    d_act = lax.dot_general(rows_grad, w_down, contract, preferred_element_type=jnp.float32)
    act, slope = silu_parts(gate_pre)
    hidden = (act * up_pre).astype(jnp.bfloat16)
    d_up = (d_act * act).astype(jnp.bfloat16)
    d_gate = (d_act * up_pre * slope).astype(jnp.bfloat16)
    grad_down = lax.dot_general(
        hidden, rows_grad, over_rows, preferred_element_type=jnp.float32
    ).astype(jnp.bfloat16)
    grad_gate = lax.dot_general(
        d_gate, rows_in, over_rows, preferred_element_type=jnp.float32
    ).astype(jnp.bfloat16)
    grad_up = lax.dot_general(d_up, rows_in, over_rows, preferred_element_type=jnp.float32).astype(
        jnp.bfloat16
    )
    pieces = jnp.dot(d_gate, w_gate, preferred_element_type=jnp.float32)
    pieces = (pieces + jnp.dot(d_up, w_up, preferred_element_type=jnp.float32)).astype(jnp.bfloat16)
    returned = lax.all_to_all(
        pieces.reshape(devices, CAP, width),
        ("node", "local"),
        split_axis=0,
        concat_axis=0,
        tiled=True,
    )
    returned = returned.reshape(devices * CAP, width)
    select_all = jnp.broadcast_to(
        select.reshape(tok_count, wave, 1, CAP), (tok_count, wave, shards, CAP)
    )
    select_all = select_all.reshape(tok_count, devices * CAP)
    grad_in = jnp.dot(select_all, returned, preferred_element_type=jnp.float32).astype(jnp.bfloat16)
    return (grad_in, grad_gate, grad_up, grad_down)


def ring_orders(count):
    order = list(range(0, count, 2)) + list(range(count - 1, 0, -2))
    ahead = [(order[i], order[(i + 1) % count]) for i in range(count)]
    behind = [(order[i], order[(i - 1) % count]) for i in range(count)]
    return ahead, behind


def dot(x, y, dims=NN):
    return lax.dot_general(x, y, dims, preferred_element_type=F32)


def held(x):
    return pltpu.with_memory_space_constraint(x, pltpu.VMEM)


def streamed(x):
    return pltpu.with_memory_space_constraint(x, pltpu.HBM)


def after(x, *earlier):
    return lax.optimization_barrier((x, *earlier))[0]


def together(*arrays):
    return lax.optimization_barrier(arrays)


def in_vmem(*shape, dtype=BF):
    return pltpu.MemorySpace.VMEM(shape, dtype)


def tiles_of(width, tile):
    return [pl.ds(k, min(tile, width - k)) for k in range(0, width, tile)]


def pick_kernel(ids_hbm, probs_hbm, samples_hbm, grad_hbm, in_hbm, mine_ref, other_ref, select_ref, *scratch):
    ids_ref, probs_ref, samples_ref, grad_ref, in_ref, sem = scratch
    sources = (ids_hbm, probs_hbm, samples_hbm, grad_hbm, in_hbm)
    copies = [pltpu.make_async_copy(x, y, sem.at[i]) for i, (x, y) in enumerate(zip(sources, scratch))]
    for copy in copies:
        copy.start()
    count = grad_ref.shape[0]
    me = lax.axis_index("node")
    upto = lax.broadcasted_iota(jnp.int32, (count, count), 0) <= lax.broadcasted_iota(
        jnp.int32, (count, count), 1
    )
    upto = upto.astype(F32).astype(BF)
    slot = lax.broadcasted_iota(jnp.int32, (CAP, count), 0).astype(F32) + 1.0
    for copy in copies[:3]:
        copy.wait()
    ids, probs = ids_ref[...], probs_ref[...]
    sample = jnp.broadcast_to(samples_ref[...].astype(F32), (count, count))
    length = jnp.sum((sample == sample.T).astype(F32), axis=0, keepdims=True)
    loss_scale = TOK_DEV / (SAMPLES * length)
    selects, factors = [], []
    for i in range(2):
        hit = ids == (me + i) % 2
        coef = jnp.sum(jnp.where(hit, probs, 0.0), axis=0, keepdims=True)
        member = jnp.max(hit.astype(F32), axis=0, keepdims=True)
        rank = dot(jnp.broadcast_to(member, (CAP, count)).astype(BF), upto)
        picked = (rank == slot) & (member > 0.0)
        selects.append(picked.astype(F32))
        factors.append(jnp.sum(jnp.where(picked, coef * loss_scale, 0.0), axis=1, keepdims=True))
    select = jnp.concatenate(selects).astype(BF)
    factor = jnp.concatenate(factors)
    select_ref[...] = select
    tiles = tiles_of(grad_ref.shape[1], 1024)
    copies[3].wait()
    for k in tiles:
        grads = (factor * dot(select, grad_ref[:, k])).astype(BF)
        mine_ref[:CAP, k] = grads[:CAP]
        other_ref[:CAP, k] = grads[CAP:]
    copies[4].wait()
    for k in tiles:
        ins = dot(select, in_ref[:, k]).astype(BF)
        mine_ref[CAP:, k] = ins[:CAP]
        other_ref[CAP:, k] = ins[CAP:]


def pick(*arrays):
    count, width = arrays[-1].shape
    return pl.pallas_call(
        pick_kernel,
        in_specs=[pl.BlockSpec(memory_space=pltpu.HBM)] * 5,
        out_specs=[IN_VMEM] * 3,
        out_shape=[in_vmem(2 * CAP, width), in_vmem(2 * CAP, width), in_vmem(2 * CAP, count)],
        scratch_shapes=[pltpu.VMEM(x.shape, x.dtype) for x in arrays] + [pltpu.SemaphoreType.DMA((5,))],
        compiler_params=pltpu.CompilerParams(vmem_limit_bytes=8 << 20),
        name="pick",
    )(*[streamed(x) for x in arrays])


def load_kernel(n, *refs):
    copies = [pltpu.make_async_copy(refs[i], refs[n + i], refs[2 * n].at[i]) for i in range(n)]
    for copy in copies:
        copy.start()
    for copy in copies:
        copy.wait()


def load(*arrays):
    n = len(arrays)
    return pl.pallas_call(
        functools.partial(load_kernel, n),
        in_specs=[pl.BlockSpec(memory_space=pltpu.HBM)] * n,
        out_specs=[IN_VMEM] * n,
        out_shape=[in_vmem(*x.shape) for x in arrays],
        scratch_shapes=[pltpu.SemaphoreType.DMA((n,))],
        cost_estimate=LIGHT,
        compiler_params=pltpu.CompilerParams(vmem_limit_bytes=1 << 20),
        name="load",
    )(*[streamed(x) for x in arrays])


def work_kernel(n, *refs):
    blocks, (gate_ref, up_ref, down_ref) = refs[:n], refs[n : n + 3]
    pieces = refs[n + 3 : 2 * n + 3]
    hidden_ref, d_up_ref, d_gate_ref, grads_ref, ins_ref = refs[2 * n + 3 :]
    for i, block in enumerate(blocks):
        rows = pl.ds(i * CAP, CAP)
        grads_ref[rows, :] = block[:CAP, :]
        ins_ref[rows, :] = block[CAP:, :]
    gate_pre = jnp.zeros((n * CAP, gate_ref.shape[0]), F32)
    up_pre = d_act = gate_pre
    for k in tiles_of(gate_ref.shape[1], 1024):
        gate_pre += dot(ins_ref[:, k], gate_ref[:, k], NT)
        up_pre += dot(ins_ref[:, k], up_ref[:, k], NT)
        d_act += dot(grads_ref[:, k], down_ref[:, k], NT)
    act, slope = silu_parts(gate_pre)
    d_up = (d_act * act).astype(BF)
    d_gate = (d_act * up_pre * slope).astype(BF)
    hidden_ref[...] = (act * up_pre).astype(BF)
    d_up_ref[...] = d_up
    d_gate_ref[...] = d_gate
    for k in tiles_of(gate_ref.shape[1], 1024):
        p = (dot(d_gate, gate_ref[:, k]) + dot(d_up, up_ref[:, k])).astype(BF)
        for i, piece in enumerate(pieces):
            piece[:, k] = p[i * CAP : (i + 1) * CAP]


def work(blocks, w_gate, w_up, w_down, flops):
    n = len(blocks)
    hid, width = w_gate.shape
    outs = [in_vmem(CAP, width)] * n + [in_vmem(n * CAP, hid)] * 3 + [in_vmem(n * CAP, width)] * 2
    out = pl.pallas_call(
        functools.partial(work_kernel, n),
        in_specs=[IN_VMEM] * (n + 3),
        out_specs=[IN_VMEM] * len(outs),
        out_shape=outs,
        cost_estimate=pl.CostEstimate(flops=flops, bytes_accessed=0, transcendentals=0),
        compiler_params=pltpu.CompilerParams(vmem_limit_bytes=4 << 20),
        name="work",
    )(*[held(x) for x in blocks], held(w_gate), held(w_up), held(w_down))
    return out[:n], out[n:]


def weight_grads_kernel(n, *refs):
    hidden, d_up, d_gate, grads, ins = (refs[i * n : (i + 1) * n] for i in range(5))
    outs, (buffer, sem) = refs[5 * n : 5 * n + 3], refs[5 * n + 3 :]
    copies = []
    for i, (left, right) in enumerate(((d_gate, ins), (d_up, ins), (hidden, grads))):
        across = jnp.concatenate([x[...] for x in left]).astype(F32).T.astype(BF)
        for k in tiles_of(buffer.shape[2], 512):
            buffer[i, :, k] = dot(across, jnp.concatenate([x[:, k] for x in right])).astype(BF)
        copies.append(pltpu.make_async_copy(buffer.at[i], outs[i], sem.at[i]))
        copies[i].start()
    for copy in copies:
        copy.wait()


def weight_grads(saved):
    n = len(saved)
    hid, width = saved[0][0].shape[1], saved[0][3].shape[1]
    return pl.pallas_call(
        functools.partial(weight_grads_kernel, n),
        in_specs=[IN_VMEM] * (5 * n),
        out_specs=[pl.BlockSpec(memory_space=pl.ANY)] * 3,
        out_shape=[jax.ShapeDtypeStruct((hid, width), BF)] * 3,
        scratch_shapes=[pltpu.VMEM((3, hid, width), BF), pltpu.SemaphoreType.DMA((3,))],
        cost_estimate=WORK_COST,
        compiler_params=pltpu.CompilerParams(vmem_limit_bytes=8 << 20),
        name="weight_grads",
    )(*[held(x) for part in zip(*saved) for x in part])


def place_kernel(select_ref, own_ref, ahead_ref, behind_ref, first_ref, second_ref, out_ref, rows_ref, buffer, sem):
    spread = select_ref[...].astype(F32).T.astype(BF)
    for k in tiles_of(out_ref.shape[1], 1024):
        here = own_ref[:, k].astype(F32) + ahead_ref[:, k].astype(F32) + behind_ref[:, k].astype(F32)
        there = first_ref[:, k].astype(F32) + second_ref[:, k].astype(F32)
        rows_ref[:CAP, k] = here.astype(BF)
        rows_ref[CAP:, k] = there.astype(BF)
    copies = []
    for j, r in enumerate(tiles_of(out_ref.shape[0], buffer.shape[0] // 2)):
        for k in tiles_of(out_ref.shape[1], 1024):
            buffer[r, k] = dot(spread[r.start : r.start + r.size], rows_ref[:, k]).astype(BF)
        copies.append(pltpu.make_async_copy(buffer.at[r], out_ref.at[r], sem.at[j]))
        copies[j].start()
    for copy in copies:
        copy.wait()


def place(select, own, ahead, behind, first, second):
    count, width = select.shape[1], own.shape[1]
    return pl.pallas_call(
        place_kernel,
        in_specs=[IN_VMEM] * 6,
        out_specs=pl.BlockSpec(memory_space=pl.ANY),
        out_shape=jax.ShapeDtypeStruct((count, width), BF),
        scratch_shapes=[pltpu.VMEM((2 * CAP, width), BF), pltpu.VMEM((count, width), BF), pltpu.SemaphoreType.DMA((2,))],
        compiler_params=pltpu.CompilerParams(vmem_limit_bytes=8 << 20),
        name="place",
    )(*[held(x) for x in (select, own, ahead, behind, first, second)])


def per_device_ring(grad_out, layer_in, expert_ids, gate_probs, sample_ids, w_gate, w_up, w_down):
    swap = [(0, 1), (1, 0)]
    ahead, behind = ring_orders(lax.axis_size("local"))
    half = lax.axis_size("local") // 2

    def go(x):
        return lax.ppermute(x, "local", ahead)

    def back(x):
        return lax.ppermute(x, "local", behind)

    def cross(x, hops):
        count = lax.axis_size("local")
        pairs = [(i * count + a, (1 - i) * count + b) for i in (0, 1) for a, b in hops]
        return lax.ppermute(x, ("node", "local"), pairs)

    near, other, select = pick(expert_ids.T, gate_probs.T, sample_ids, grad_out, layer_in)
    far = lax.ppermute(other, "node", swap)

    weights = load(w_gate, w_up, w_down)
    saved = []
    pieces = {}

    def work_on(members, flops=0):
        outs, keep = work([rows[member] for member in members], *weights, flops)
        pieces.update(zip(members, outs))
        saved.append(keep)
        return keep[0]

    rows = {(0, 0): near, (0, 1): far}
    near_go, near_back, far_go, far_back = near, near, far, far
    for s in range(1, half):
        near_go, near_back = go(near_go), back(near_back)
        if s == 2:
            far_go, far_back = after(far_go, weights[0]), after(far_back, weights[0])
        far_go, far_back = go(far_go), back(far_back)
        rows.update({(-s, 0): near_go, (s, 0): near_back, (-s, 1): far_go, (s, 1): far_back})
        if s == half - 2:
            done = work_on(list(rows)[:-2], 3000000000)
            far_go, far_back = after(far_go, done), after(far_back, done)
    near_go, near_back = together(near_go, near_back)
    far_go, far_back = together(far_go, far_back)
    last_near = jnp.concatenate([go(near_go[:CAP]), back(near_back[CAP:])])
    last_far = jnp.concatenate([go(far_go[:CAP]), back(far_back[CAP:])])
    rows.update({(half, 0): last_near, (half, 1): last_far})
    work_on([member for member in rows if member not in pieces], 0)

    def add(x, y):
        return (x.astype(F32) + y.astype(F32)).astype(BF)

    far_long, near_long = pieces[half, 1], pieces[half, 0]
    far_short, near_short = pieces[half - 1, 1], pieces[1 - half, 0]
    for s in range(half - 1, 0, -1):
        far_long, near_long = back(far_long), go(near_long)
        far_short, near_short = go(far_short), back(near_short)
        far_long, near_long = add(pieces[-s, 1], far_long), add(pieces[s, 0], near_long)
        if s > 1:
            far_short, near_short = add(pieces[s - 1, 1], far_short), add(pieces[1 - s, 0], near_short)
            far_short, near_short = after(far_short, far_long), after(near_short, near_long)
    saved[0] = [after(saved[0][0], far_long, near_long), *saved[0][1:]]
    grad_gate, grad_up, grad_down = weight_grads(saved)
    far_long, near_long = cross(far_long, behind), go(near_long)
    first = lax.ppermute(add(pieces[0, 1], far_short), "node", swap)
    grad_in = place(select, pieces[0, 0], near_long, near_short, first, far_long)
    return (grad_in, grad_gate, grad_up, grad_down)


def solution(mesh):
    nodes, locals_ = mesh.shape["node"], mesh.shape["local"]
    ring = nodes == 2 and locals_ % 2 == 0 and locals_ >= 8

    def per_device(*args):
        shards = FF // args[5].shape[0]
        if ring and shards == locals_:
            return per_device_ring(*args)
        return per_device_exchange(*args)

    return jax.shard_map(
        per_device,
        mesh=mesh,
        in_specs=(
            P(("groups", "node", "local"), None),
            P(("groups", "node", "local"), None),
            P(("groups", "node", "local"), None),
            P(("groups", "node", "local"), None),
            P(("groups", "node", "local"), None),
            P(("node", "local"), None),
            P(("node", "local"), None),
            P(("node", "local"), None),
        ),
        out_specs=(
            P(("groups", "node", "local"), None),
            P(("groups", "node", "local"), None),
            P(("groups", "node", "local"), None),
            P(("groups", "node", "local"), None),
        ),
        check_vma=False,
    )
```

```python
import functools

import jax
import jax.numpy as jnp
from jax import lax
from jax.experimental import pallas as pl
from jax.experimental.pallas import tpu as pltpu
from jax.sharding import PartitionSpec as P

FF = 1536
SAMPLES = 8
TOK_DEV = 128
CAP = 16
BF = jnp.bfloat16
WORK_COST = pl.CostEstimate(flops=3000000000, bytes_accessed=0, transcendentals=0)
F32 = jnp.float32
NT = (((1,), (1,)), ((), ()))
TN = (((0,), (0,)), ((), ()))
NN = (((1,), (0,)), ((), ()))
IN_VMEM = pl.BlockSpec(memory_space=pltpu.VMEM)
LIGHT = pl.CostEstimate(flops=0, bytes_accessed=0, transcendentals=0)


def silu_parts(pre):
    sigma = jax.nn.sigmoid(pre)
    return (pre * sigma, sigma * (1.0 + pre * (1.0 - sigma)))


def per_device_exchange(grad_out, layer_in, expert_ids, gate_probs, sample_ids, w_gate, w_up, w_down):
    tok_count = grad_out.shape[0]
    width = grad_out.shape[1]
    shard_width = w_gate.shape[0]
    node_count = lax.axis_size("node")
    local_count = lax.axis_size("local")
    devices = node_count * local_count
    shards = FF // shard_width
    wave = devices // shards
    contract = (((1,), (1,)), ((), ()))
    over_rows = (((0,), (0,)), ((), ()))
    packed = sample_ids[0]
    same_sample = packed[:, None] == packed[None, :]
    length = jnp.sum(same_sample.astype(jnp.int32), axis=1)
    loss_scale = TOK_DEV / (SAMPLES * length.astype(jnp.float32))
    expert_range = jnp.arange(wave, dtype=jnp.int32)
    hit = expert_ids[:, :, None] == expert_range[None, None, :]
    coef = jnp.sum(jnp.where(hit, gate_probs[:, :, None], 0.0), axis=1)
    member = jnp.any(hit, axis=1).astype(jnp.int32)
    rank = jnp.cumsum(member, axis=0) - 1
    slot_range = jnp.arange(CAP, dtype=jnp.int32)
    picked = (member[:, :, None] == 1) & (rank[:, :, None] == slot_range[None, None, :])
    factor = coef * loss_scale[:, None]
    slot_factor = jnp.sum(jnp.where(picked, factor[:, :, None], 0.0), axis=0).reshape(wave * CAP, 1)
    select = picked.astype(jnp.bfloat16).reshape(tok_count, wave * CAP)
    chosen_grad = lax.dot_general(select, grad_out, over_rows, preferred_element_type=jnp.float32)
    send_grad = (slot_factor * chosen_grad).astype(jnp.bfloat16)
    send_in = lax.dot_general(
        select, layer_in, over_rows, preferred_element_type=jnp.float32
    ).astype(jnp.bfloat16)
    flat_grad = jnp.broadcast_to(
        send_grad.reshape(wave, 1, CAP, width), (wave, shards, CAP, width)
    ).reshape(devices, CAP, width)
    flat_in = jnp.broadcast_to(
        send_in.reshape(wave, 1, CAP, width), (wave, shards, CAP, width)
    ).reshape(devices, CAP, width)
    recv_grad, recv_in = (
        lax.all_to_all(flat_grad, ("node", "local"), split_axis=0, concat_axis=0, tiled=True),
        lax.all_to_all(flat_in, ("node", "local"), split_axis=0, concat_axis=0, tiled=True),
    )
    rows_grad = recv_grad.reshape(devices * CAP, width)
    rows_in = recv_in.reshape(devices * CAP, width)
    gate_pre = lax.dot_general(rows_in, w_gate, contract, preferred_element_type=jnp.float32)
    up_pre = lax.dot_general(rows_in, w_up, contract, preferred_element_type=jnp.float32)
    d_act = lax.dot_general(rows_grad, w_down, contract, preferred_element_type=jnp.float32)
    act, slope = silu_parts(gate_pre)
    hidden = (act * up_pre).astype(jnp.bfloat16)
    d_up = (d_act * act).astype(jnp.bfloat16)
    d_gate = (d_act * up_pre * slope).astype(jnp.bfloat16)
    grad_down = lax.dot_general(
        hidden, rows_grad, over_rows, preferred_element_type=jnp.float32
    ).astype(jnp.bfloat16)
    grad_gate = lax.dot_general(
        d_gate, rows_in, over_rows, preferred_element_type=jnp.float32
    ).astype(jnp.bfloat16)
    grad_up = lax.dot_general(d_up, rows_in, over_rows, preferred_element_type=jnp.float32).astype(
        jnp.bfloat16
    )
    pieces = jnp.dot(d_gate, w_gate, preferred_element_type=jnp.float32)
    pieces = (pieces + jnp.dot(d_up, w_up, preferred_element_type=jnp.float32)).astype(jnp.bfloat16)
    returned = lax.all_to_all(
        pieces.reshape(devices, CAP, width),
        ("node", "local"),
        split_axis=0,
        concat_axis=0,
        tiled=True,
    )
    returned = returned.reshape(devices * CAP, width)
    select_all = jnp.broadcast_to(
        select.reshape(tok_count, wave, 1, CAP), (tok_count, wave, shards, CAP)
    )
    select_all = select_all.reshape(tok_count, devices * CAP)
    grad_in = jnp.dot(select_all, returned, preferred_element_type=jnp.float32).astype(jnp.bfloat16)
    return (grad_in, grad_gate, grad_up, grad_down)


def ring_orders(count):
    order = list(range(0, count, 2)) + list(range(count - 1, 0, -2))
    ahead = [(order[i], order[(i + 1) % count]) for i in range(count)]
    behind = [(order[i], order[(i - 1) % count]) for i in range(count)]
    return ahead, behind


def dot(x, y, dims=NN):
    return lax.dot_general(x, y, dims, preferred_element_type=F32)


def held(x):
    return pltpu.with_memory_space_constraint(x, pltpu.VMEM)


def streamed(x):
    return pltpu.with_memory_space_constraint(x, pltpu.HBM)


def after(x, *earlier):
    return lax.optimization_barrier((x, *earlier))[0]


def together(*arrays):
    return lax.optimization_barrier(arrays)


def in_vmem(*shape, dtype=BF):
    return pltpu.MemorySpace.VMEM(shape, dtype)


def tiles_of(width, tile):
    return [pl.ds(k, min(tile, width - k)) for k in range(0, width, tile)]


def pick_kernel(ids_hbm, probs_hbm, samples_hbm, grad_hbm, in_hbm, mine_ref, other_ref, select_ref, *scratch):
    ids_ref, probs_ref, samples_ref, grad_ref, in_ref, sem = scratch
    sources = (ids_hbm, probs_hbm, samples_hbm, grad_hbm, in_hbm)
    copies = [pltpu.make_async_copy(x, y, sem.at[i]) for i, (x, y) in enumerate(zip(sources, scratch))]
    for copy in copies:
        copy.start()
    count = grad_ref.shape[0]
    me = lax.axis_index("node")
    upto = lax.broadcasted_iota(jnp.int32, (count, count), 0) <= lax.broadcasted_iota(
        jnp.int32, (count, count), 1
    )
    upto = upto.astype(F32).astype(BF)
    slot = lax.broadcasted_iota(jnp.int32, (CAP, count), 0).astype(F32) + 1.0
    for copy in copies[:3]:
        copy.wait()
    ids, probs = ids_ref[...], probs_ref[...]
    sample = jnp.broadcast_to(samples_ref[...].astype(F32), (count, count))
    length = jnp.sum((sample == sample.T).astype(F32), axis=0, keepdims=True)
    loss_scale = TOK_DEV / (SAMPLES * length)
    selects, factors = [], []
    for i in range(2):
        hit = ids == (me + i) % 2
        coef = jnp.sum(jnp.where(hit, probs, 0.0), axis=0, keepdims=True)
        member = jnp.max(hit.astype(F32), axis=0, keepdims=True)
        rank = dot(jnp.broadcast_to(member, (CAP, count)).astype(BF), upto)
        picked = (rank == slot) & (member > 0.0)
        selects.append(picked.astype(F32))
        factors.append(jnp.sum(jnp.where(picked, coef * loss_scale, 0.0), axis=1, keepdims=True))
    select = jnp.concatenate(selects).astype(BF)
    factor = jnp.concatenate(factors)
    select_ref[...] = select
    tiles = tiles_of(grad_ref.shape[1], 1024)
    copies[3].wait()
    for k in tiles:
        grads = (factor * dot(select, grad_ref[:, k])).astype(BF)
        mine_ref[:CAP, k] = grads[:CAP]
        other_ref[:CAP, k] = grads[CAP:]
    copies[4].wait()
    for k in tiles:
        ins = dot(select, in_ref[:, k]).astype(BF)
        mine_ref[CAP:, k] = ins[:CAP]
        other_ref[CAP:, k] = ins[CAP:]


def pick(*arrays):
    count, width = arrays[-1].shape
    return pl.pallas_call(
        pick_kernel,
        in_specs=[pl.BlockSpec(memory_space=pltpu.HBM)] * 5,
        out_specs=[IN_VMEM] * 3,
        out_shape=[in_vmem(2 * CAP, width), in_vmem(2 * CAP, width), in_vmem(2 * CAP, count)],
        scratch_shapes=[pltpu.VMEM(x.shape, x.dtype) for x in arrays] + [pltpu.SemaphoreType.DMA((5,))],
        compiler_params=pltpu.CompilerParams(vmem_limit_bytes=8 << 20),
        name="pick",
    )(*[streamed(x) for x in arrays])


def load_kernel(n, *refs):
    copies = [pltpu.make_async_copy(refs[i], refs[n + i], refs[2 * n].at[i]) for i in range(n)]
    for copy in copies:
        copy.start()
    for copy in copies:
        copy.wait()


def load(*arrays):
    n = len(arrays)
    return pl.pallas_call(
        functools.partial(load_kernel, n),
        in_specs=[pl.BlockSpec(memory_space=pltpu.HBM)] * n,
        out_specs=[IN_VMEM] * n,
        out_shape=[in_vmem(*x.shape) for x in arrays],
        scratch_shapes=[pltpu.SemaphoreType.DMA((n,))],
        cost_estimate=LIGHT,
        compiler_params=pltpu.CompilerParams(vmem_limit_bytes=1 << 20),
        name="load",
    )(*[streamed(x) for x in arrays])


def work_kernel(n, *refs):
    blocks, (gate_ref, up_ref, down_ref) = refs[:n], refs[n : n + 3]
    pieces = refs[n + 3 : 2 * n + 3]
    hidden_ref, d_up_ref, d_gate_ref, grads_ref, ins_ref = refs[2 * n + 3 :]
    for i, block in enumerate(blocks):
        rows = pl.ds(i * CAP, CAP)
        grads_ref[rows, :] = block[:CAP, :]
        ins_ref[rows, :] = block[CAP:, :]
    gate_pre = jnp.zeros((n * CAP, gate_ref.shape[0]), F32)
    up_pre = d_act = gate_pre
    for k in tiles_of(gate_ref.shape[1], 1024):
        gate_pre += dot(ins_ref[:, k], gate_ref[:, k], NT)
        up_pre += dot(ins_ref[:, k], up_ref[:, k], NT)
        d_act += dot(grads_ref[:, k], down_ref[:, k], NT)
    act, slope = silu_parts(gate_pre)
    d_up = (d_act * act).astype(BF)
    d_gate = (d_act * up_pre * slope).astype(BF)
    hidden_ref[...] = (act * up_pre).astype(BF)
    d_up_ref[...] = d_up
    d_gate_ref[...] = d_gate
    for k in tiles_of(gate_ref.shape[1], 1024):
        p = (dot(d_gate, gate_ref[:, k]) + dot(d_up, up_ref[:, k])).astype(BF)
        for i, piece in enumerate(pieces):
            piece[:, k] = p[i * CAP : (i + 1) * CAP]


def work(blocks, w_gate, w_up, w_down, flops):
    n = len(blocks)
    hid, width = w_gate.shape
    outs = [in_vmem(CAP, width)] * n + [in_vmem(n * CAP, hid)] * 3 + [in_vmem(n * CAP, width)] * 2
    out = pl.pallas_call(
        functools.partial(work_kernel, n),
        in_specs=[IN_VMEM] * (n + 3),
        out_specs=[IN_VMEM] * len(outs),
        out_shape=outs,
        cost_estimate=pl.CostEstimate(flops=flops, bytes_accessed=0, transcendentals=0),
        compiler_params=pltpu.CompilerParams(vmem_limit_bytes=4 << 20),
        name="work",
    )(*[held(x) for x in blocks], held(w_gate), held(w_up), held(w_down))
    return out[:n], out[n:]


def weight_grads_kernel(n, *refs):
    hidden, d_up, d_gate, grads, ins = (refs[i * n : (i + 1) * n] for i in range(5))
    outs, (buffer, sem) = refs[5 * n : 5 * n + 3], refs[5 * n + 3 :]
    copies = []
    for i, (left, right) in enumerate(((d_gate, ins), (d_up, ins), (hidden, grads))):
        across = jnp.concatenate([x[...] for x in left]).astype(F32).T.astype(BF)
        for k in tiles_of(buffer.shape[2], 512):
            buffer[i, :, k] = dot(across, jnp.concatenate([x[:, k] for x in right])).astype(BF)
        copies.append(pltpu.make_async_copy(buffer.at[i], outs[i], sem.at[i]))
        copies[i].start()
    for copy in copies:
        copy.wait()


def weight_grads(saved):
    n = len(saved)
    hid, width = saved[0][0].shape[1], saved[0][3].shape[1]
    return pl.pallas_call(
        functools.partial(weight_grads_kernel, n),
        in_specs=[IN_VMEM] * (5 * n),
        out_specs=[pl.BlockSpec(memory_space=pl.ANY)] * 3,
        out_shape=[jax.ShapeDtypeStruct((hid, width), BF)] * 3,
        scratch_shapes=[pltpu.VMEM((3, hid, width), BF), pltpu.SemaphoreType.DMA((3,))],
        cost_estimate=WORK_COST,
        compiler_params=pltpu.CompilerParams(vmem_limit_bytes=8 << 20),
        name="weight_grads",
    )(*[held(x) for part in zip(*saved) for x in part])


def place_kernel(select_ref, own_ref, ahead_ref, behind_ref, first_ref, second_ref, out_ref, rows_ref, buffer, sem):
    spread = select_ref[...].astype(F32).T.astype(BF)
    for k in tiles_of(out_ref.shape[1], 1024):
        here = own_ref[:, k].astype(F32) + ahead_ref[:, k].astype(F32) + behind_ref[:, k].astype(F32)
        there = first_ref[:, k].astype(F32) + second_ref[:, k].astype(F32)
        rows_ref[:CAP, k] = here.astype(BF)
        rows_ref[CAP:, k] = there.astype(BF)
    copies = []
    for j, r in enumerate(tiles_of(out_ref.shape[0], buffer.shape[0] // 4)):
        for k in tiles_of(out_ref.shape[1], 1024):
            buffer[r, k] = dot(spread[r.start : r.start + r.size], rows_ref[:, k]).astype(BF)
        copies.append(pltpu.make_async_copy(buffer.at[r], out_ref.at[r], sem.at[j]))
        copies[j].start()
    for copy in copies:
        copy.wait()


def place(select, own, ahead, behind, first, second):
    count, width = select.shape[1], own.shape[1]
    return pl.pallas_call(
        place_kernel,
        in_specs=[IN_VMEM] * 6,
        out_specs=pl.BlockSpec(memory_space=pl.ANY),
        out_shape=jax.ShapeDtypeStruct((count, width), BF),
        scratch_shapes=[pltpu.VMEM((2 * CAP, width), BF), pltpu.VMEM((count, width), BF), pltpu.SemaphoreType.DMA((4,))],
        compiler_params=pltpu.CompilerParams(vmem_limit_bytes=8 << 20),
        name="place",
    )(*[held(x) for x in (select, own, ahead, behind, first, second)])


def per_device_ring(grad_out, layer_in, expert_ids, gate_probs, sample_ids, w_gate, w_up, w_down):
    swap = [(0, 1), (1, 0)]
    ahead, behind = ring_orders(lax.axis_size("local"))
    half = lax.axis_size("local") // 2

    def go(x):
        return lax.ppermute(x, "local", ahead)

    def back(x):
        return lax.ppermute(x, "local", behind)

    def cross(x, hops):
        count = lax.axis_size("local")
        pairs = [(i * count + a, (1 - i) * count + b) for i in (0, 1) for a, b in hops]
        return lax.ppermute(x, ("node", "local"), pairs)

    near, other, select = pick(expert_ids.T, gate_probs.T, sample_ids, grad_out, layer_in)
    far = lax.ppermute(other, "node", swap)

    weights = load(w_gate, w_up, w_down)
    saved = []
    pieces = {}

    def work_on(members, flops=0):
        outs, keep = work([rows[member] for member in members], *weights, flops)
        pieces.update(zip(members, outs))
        saved.append(keep)
        return keep[0]

    rows = {(0, 0): near, (0, 1): far}
    near_go, near_back, far_go, far_back = near, near, far, far
    for s in range(1, half):
        near_go, near_back = go(near_go), back(near_back)
        if s == 2:
            far_go, far_back = after(far_go, weights[0]), after(far_back, weights[0])
        far_go, far_back = go(far_go), back(far_back)
        rows.update({(-s, 0): near_go, (s, 0): near_back, (-s, 1): far_go, (s, 1): far_back})
        if s == half - 2:
            done = work_on(list(rows)[:-2], 3000000000)
            far_go, far_back = after(far_go, done), after(far_back, done)
    near_go, near_back = together(near_go, near_back)
    far_go, far_back = together(far_go, far_back)
    last_near = jnp.concatenate([go(near_go[:CAP]), back(near_back[CAP:])])
    last_far = jnp.concatenate([go(far_go[:CAP]), back(far_back[CAP:])])
    rows.update({(half, 0): last_near, (half, 1): last_far})
    work_on([member for member in rows if member not in pieces], 0)

    def add(x, y):
        return (x.astype(F32) + y.astype(F32)).astype(BF)

    far_long, near_long = pieces[half, 1], pieces[half, 0]
    far_short, near_short = pieces[half - 1, 1], pieces[1 - half, 0]
    for s in range(half - 1, 0, -1):
        far_long, near_long = back(far_long), go(near_long)
        far_short, near_short = go(far_short), back(near_short)
        far_long, near_long = add(pieces[-s, 1], far_long), add(pieces[s, 0], near_long)
        if s > 1:
            far_short, near_short = add(pieces[s - 1, 1], far_short), add(pieces[1 - s, 0], near_short)
    saved[0] = [after(saved[0][0], far_long, near_long), *saved[0][1:]]
    grad_gate, grad_up, grad_down = weight_grads(saved)
    far_long, near_long = cross(far_long, behind), go(near_long)
    first = lax.ppermute(add(pieces[0, 1], far_short), "node", swap)
    grad_in = place(select, pieces[0, 0], near_long, near_short, first, far_long)
    return (grad_in, grad_gate, grad_up, grad_down)


def solution(mesh):
    nodes, locals_ = mesh.shape["node"], mesh.shape["local"]
    ring = nodes == 2 and locals_ % 2 == 0 and locals_ >= 8

    def per_device(*args):
        shards = FF // args[5].shape[0]
        if ring and shards == locals_:
            return per_device_ring(*args)
        return per_device_exchange(*args)

    return jax.shard_map(
        per_device,
        mesh=mesh,
        in_specs=(
            P(("groups", "node", "local"), None),
            P(("groups", "node", "local"), None),
            P(("groups", "node", "local"), None),
            P(("groups", "node", "local"), None),
            P(("groups", "node", "local"), None),
            P(("node", "local"), None),
            P(("node", "local"), None),
            P(("node", "local"), None),
        ),
        out_specs=(
            P(("groups", "node", "local"), None),
            P(("groups", "node", "local"), None),
            P(("groups", "node", "local"), None),
            P(("groups", "node", "local"), None),
        ),
        check_vma=False,
    )
```

```python
import functools

import jax
import jax.numpy as jnp
from jax import lax
from jax.experimental import pallas as pl
from jax.experimental.pallas import tpu as pltpu
from jax.sharding import PartitionSpec as P

FF = 1536
SAMPLES = 8
TOK_DEV = 128
CAP = 16
BF = jnp.bfloat16
WORK_COST = pl.CostEstimate(flops=3000000000, bytes_accessed=0, transcendentals=0)
F32 = jnp.float32
NT = (((1,), (1,)), ((), ()))
TN = (((0,), (0,)), ((), ()))
NN = (((1,), (0,)), ((), ()))
IN_VMEM = pl.BlockSpec(memory_space=pltpu.VMEM)
LIGHT = pl.CostEstimate(flops=0, bytes_accessed=0, transcendentals=0)


def silu_parts(pre):
    sigma = jax.nn.sigmoid(pre)
    return (pre * sigma, sigma * (1.0 + pre * (1.0 - sigma)))


def per_device_exchange(grad_out, layer_in, expert_ids, gate_probs, sample_ids, w_gate, w_up, w_down):
    tok_count = grad_out.shape[0]
    width = grad_out.shape[1]
    shard_width = w_gate.shape[0]
    node_count = lax.axis_size("node")
    local_count = lax.axis_size("local")
    devices = node_count * local_count
    shards = FF // shard_width
    wave = devices // shards
    contract = (((1,), (1,)), ((), ()))
    over_rows = (((0,), (0,)), ((), ()))
    packed = sample_ids[0]
    same_sample = packed[:, None] == packed[None, :]
    length = jnp.sum(same_sample.astype(jnp.int32), axis=1)
    loss_scale = TOK_DEV / (SAMPLES * length.astype(jnp.float32))
    expert_range = jnp.arange(wave, dtype=jnp.int32)
    hit = expert_ids[:, :, None] == expert_range[None, None, :]
    coef = jnp.sum(jnp.where(hit, gate_probs[:, :, None], 0.0), axis=1)
    member = jnp.any(hit, axis=1).astype(jnp.int32)
    rank = jnp.cumsum(member, axis=0) - 1
    slot_range = jnp.arange(CAP, dtype=jnp.int32)
    picked = (member[:, :, None] == 1) & (rank[:, :, None] == slot_range[None, None, :])
    factor = coef * loss_scale[:, None]
    slot_factor = jnp.sum(jnp.where(picked, factor[:, :, None], 0.0), axis=0).reshape(wave * CAP, 1)
    select = picked.astype(jnp.bfloat16).reshape(tok_count, wave * CAP)
    chosen_grad = lax.dot_general(select, grad_out, over_rows, preferred_element_type=jnp.float32)
    send_grad = (slot_factor * chosen_grad).astype(jnp.bfloat16)
    send_in = lax.dot_general(
        select, layer_in, over_rows, preferred_element_type=jnp.float32
    ).astype(jnp.bfloat16)
    flat_grad = jnp.broadcast_to(
        send_grad.reshape(wave, 1, CAP, width), (wave, shards, CAP, width)
    ).reshape(devices, CAP, width)
    flat_in = jnp.broadcast_to(
        send_in.reshape(wave, 1, CAP, width), (wave, shards, CAP, width)
    ).reshape(devices, CAP, width)
    recv_grad, recv_in = (
        lax.all_to_all(flat_grad, ("node", "local"), split_axis=0, concat_axis=0, tiled=True),
        lax.all_to_all(flat_in, ("node", "local"), split_axis=0, concat_axis=0, tiled=True),
    )
    rows_grad = recv_grad.reshape(devices * CAP, width)
    rows_in = recv_in.reshape(devices * CAP, width)
    gate_pre = lax.dot_general(rows_in, w_gate, contract, preferred_element_type=jnp.float32)
    up_pre = lax.dot_general(rows_in, w_up, contract, preferred_element_type=jnp.float32)
    d_act = lax.dot_general(rows_grad, w_down, contract, preferred_element_type=jnp.float32)
    act, slope = silu_parts(gate_pre)
    hidden = (act * up_pre).astype(jnp.bfloat16)
    d_up = (d_act * act).astype(jnp.bfloat16)
    d_gate = (d_act * up_pre * slope).astype(jnp.bfloat16)
    grad_down = lax.dot_general(
        hidden, rows_grad, over_rows, preferred_element_type=jnp.float32
    ).astype(jnp.bfloat16)
    grad_gate = lax.dot_general(
        d_gate, rows_in, over_rows, preferred_element_type=jnp.float32
    ).astype(jnp.bfloat16)
    grad_up = lax.dot_general(d_up, rows_in, over_rows, preferred_element_type=jnp.float32).astype(
        jnp.bfloat16
    )
    pieces = jnp.dot(d_gate, w_gate, preferred_element_type=jnp.float32)
    pieces = (pieces + jnp.dot(d_up, w_up, preferred_element_type=jnp.float32)).astype(jnp.bfloat16)
    returned = lax.all_to_all(
        pieces.reshape(devices, CAP, width),
        ("node", "local"),
        split_axis=0,
        concat_axis=0,
        tiled=True,
    )
    returned = returned.reshape(devices * CAP, width)
    select_all = jnp.broadcast_to(
        select.reshape(tok_count, wave, 1, CAP), (tok_count, wave, shards, CAP)
    )
    select_all = select_all.reshape(tok_count, devices * CAP)
    grad_in = jnp.dot(select_all, returned, preferred_element_type=jnp.float32).astype(jnp.bfloat16)
    return (grad_in, grad_gate, grad_up, grad_down)


def ring_orders(count):
    order = list(range(0, count, 2)) + list(range(count - 1, 0, -2))
    ahead = [(order[i], order[(i + 1) % count]) for i in range(count)]
    behind = [(order[i], order[(i - 1) % count]) for i in range(count)]
    return ahead, behind


def dot(x, y, dims=NN):
    return lax.dot_general(x, y, dims, preferred_element_type=F32)


def held(x):
    return pltpu.with_memory_space_constraint(x, pltpu.VMEM)


def streamed(x):
    return pltpu.with_memory_space_constraint(x, pltpu.HBM)


def after(x, *earlier):
    return lax.optimization_barrier((x, *earlier))[0]


def together(*arrays):
    return lax.optimization_barrier(arrays)


def in_vmem(*shape, dtype=BF):
    return pltpu.MemorySpace.VMEM(shape, dtype)


def tiles_of(width, tile):
    return [pl.ds(k, min(tile, width - k)) for k in range(0, width, tile)]


def pick_kernel(ids_hbm, probs_hbm, samples_hbm, grad_hbm, in_hbm, mine_ref, other_ref, select_ref, *scratch):
    ids_ref, probs_ref, samples_ref, grad_ref, in_ref, sem = scratch
    sources = (ids_hbm, probs_hbm, samples_hbm, grad_hbm, in_hbm)
    copies = [pltpu.make_async_copy(x, y, sem.at[i]) for i, (x, y) in enumerate(zip(sources, scratch))]
    for copy in copies:
        copy.start()
    count = grad_ref.shape[0]
    me = lax.axis_index("node")
    upto = lax.broadcasted_iota(jnp.int32, (count, count), 0) <= lax.broadcasted_iota(
        jnp.int32, (count, count), 1
    )
    upto = upto.astype(F32).astype(BF)
    slot = lax.broadcasted_iota(jnp.int32, (CAP, count), 0).astype(F32) + 1.0
    for copy in copies[:3]:
        copy.wait()
    ids, probs = ids_ref[...], probs_ref[...]
    sample = jnp.broadcast_to(samples_ref[...].astype(F32), (count, count))
    length = jnp.sum((sample == sample.T).astype(F32), axis=0, keepdims=True)
    loss_scale = TOK_DEV / (SAMPLES * length)
    selects, factors = [], []
    for i in range(2):
        hit = ids == (me + i) % 2
        coef = jnp.sum(jnp.where(hit, probs, 0.0), axis=0, keepdims=True)
        member = jnp.max(hit.astype(F32), axis=0, keepdims=True)
        rank = dot(jnp.broadcast_to(member, (CAP, count)).astype(BF), upto)
        picked = (rank == slot) & (member > 0.0)
        selects.append(picked.astype(F32))
        factors.append(jnp.sum(jnp.where(picked, coef * loss_scale, 0.0), axis=1, keepdims=True))
    select = jnp.concatenate(selects).astype(BF)
    factor = jnp.concatenate(factors)
    select_ref[...] = select
    tiles = tiles_of(grad_ref.shape[1], 1024)
    copies[3].wait()
    for k in tiles:
        grads = (factor * dot(select, grad_ref[:, k])).astype(BF)
        mine_ref[:CAP, k] = grads[:CAP]
        other_ref[:CAP, k] = grads[CAP:]
    copies[4].wait()
    for k in tiles:
        ins = dot(select, in_ref[:, k]).astype(BF)
        mine_ref[CAP:, k] = ins[:CAP]
        other_ref[CAP:, k] = ins[CAP:]


def pick(*arrays):
    count, width = arrays[-1].shape
    return pl.pallas_call(
        pick_kernel,
        in_specs=[pl.BlockSpec(memory_space=pltpu.HBM)] * 5,
        out_specs=[IN_VMEM] * 3,
        out_shape=[in_vmem(2 * CAP, width), in_vmem(2 * CAP, width), in_vmem(2 * CAP, count)],
        scratch_shapes=[pltpu.VMEM(x.shape, x.dtype) for x in arrays] + [pltpu.SemaphoreType.DMA((5,))],
        compiler_params=pltpu.CompilerParams(vmem_limit_bytes=8 << 20),
        name="pick",
    )(*[streamed(x) for x in arrays])


def load_kernel(n, *refs):
    copies = [pltpu.make_async_copy(refs[i], refs[n + i], refs[2 * n].at[i]) for i in range(n)]
    for copy in copies:
        copy.start()
    for copy in copies:
        copy.wait()


def load(*arrays):
    n = len(arrays)
    return pl.pallas_call(
        functools.partial(load_kernel, n),
        in_specs=[pl.BlockSpec(memory_space=pltpu.HBM)] * n,
        out_specs=[IN_VMEM] * n,
        out_shape=[in_vmem(*x.shape) for x in arrays],
        scratch_shapes=[pltpu.SemaphoreType.DMA((n,))],
        cost_estimate=LIGHT,
        compiler_params=pltpu.CompilerParams(vmem_limit_bytes=1 << 20),
        name="load",
    )(*[streamed(x) for x in arrays])


def work_kernel(n, *refs):
    blocks, (gate_ref, up_ref, down_ref) = refs[:n], refs[n : n + 3]
    pieces = refs[n + 3 : 2 * n + 3]
    hidden_ref, d_up_ref, d_gate_ref, grads_ref, ins_ref = refs[2 * n + 3 :]
    for i, block in enumerate(blocks):
        rows = pl.ds(i * CAP, CAP)
        grads_ref[rows, :] = block[:CAP, :]
        ins_ref[rows, :] = block[CAP:, :]
    gate_pre = jnp.zeros((n * CAP, gate_ref.shape[0]), F32)
    up_pre = d_act = gate_pre
    for k in tiles_of(gate_ref.shape[1], 1024):
        gate_pre += dot(ins_ref[:, k], gate_ref[:, k], NT)
        up_pre += dot(ins_ref[:, k], up_ref[:, k], NT)
        d_act += dot(grads_ref[:, k], down_ref[:, k], NT)
    act, slope = silu_parts(gate_pre)
    d_up = (d_act * act).astype(BF)
    d_gate = (d_act * up_pre * slope).astype(BF)
    hidden_ref[...] = (act * up_pre).astype(BF)
    d_up_ref[...] = d_up
    d_gate_ref[...] = d_gate
    for k in tiles_of(gate_ref.shape[1], 1024):
        p = (dot(d_gate, gate_ref[:, k]) + dot(d_up, up_ref[:, k])).astype(BF)
        for i, piece in enumerate(pieces):
            piece[:, k] = p[i * CAP : (i + 1) * CAP]


def work(blocks, w_gate, w_up, w_down, flops):
    n = len(blocks)
    hid, width = w_gate.shape
    outs = [in_vmem(CAP, width)] * n + [in_vmem(n * CAP, hid)] * 3 + [in_vmem(n * CAP, width)] * 2
    out = pl.pallas_call(
        functools.partial(work_kernel, n),
        in_specs=[IN_VMEM] * (n + 3),
        out_specs=[IN_VMEM] * len(outs),
        out_shape=outs,
        cost_estimate=pl.CostEstimate(flops=flops, bytes_accessed=0, transcendentals=0),
        compiler_params=pltpu.CompilerParams(vmem_limit_bytes=4 << 20),
        name="work",
    )(*[held(x) for x in blocks], held(w_gate), held(w_up), held(w_down))
    return out[:n], out[n:]


def weight_grads_kernel(n, *refs):
    hidden, d_up, d_gate, grads, ins = (refs[i * n : (i + 1) * n] for i in range(5))
    outs, (buffer, sem) = refs[5 * n : 5 * n + 3], refs[5 * n + 3 :]
    copies = []
    for i, (left, right) in enumerate(((d_gate, ins), (d_up, ins), (hidden, grads))):
        across = jnp.concatenate([x[...] for x in left]).astype(F32).T.astype(BF)
        for k in tiles_of(buffer.shape[2], 512):
            buffer[i, :, k] = dot(across, jnp.concatenate([x[:, k] for x in right])).astype(BF)
        copies.append(pltpu.make_async_copy(buffer.at[i], outs[i], sem.at[i]))
        copies[i].start()
    for copy in copies:
        copy.wait()


def weight_grads(saved):
    n = len(saved)
    hid, width = saved[0][0].shape[1], saved[0][3].shape[1]
    return pl.pallas_call(
        functools.partial(weight_grads_kernel, n),
        in_specs=[IN_VMEM] * (5 * n),
        out_specs=[pl.BlockSpec(memory_space=pl.ANY)] * 3,
        out_shape=[jax.ShapeDtypeStruct((hid, width), BF)] * 3,
        scratch_shapes=[pltpu.VMEM((3, hid, width), BF), pltpu.SemaphoreType.DMA((3,))],
        cost_estimate=WORK_COST,
        compiler_params=pltpu.CompilerParams(vmem_limit_bytes=8 << 20),
        name="weight_grads",
    )(*[held(x) for part in zip(*saved) for x in part])


def place_kernel(select_ref, own_ref, ahead_ref, behind_ref, first_ref, second_ref, out_ref, rows_ref, buffer, sem):
    spread = select_ref[...].astype(F32).T.astype(BF)
    for k in tiles_of(out_ref.shape[1], 1024):
        here = own_ref[:, k].astype(F32) + ahead_ref[:, k].astype(F32) + behind_ref[:, k].astype(F32)
        there = first_ref[:, k].astype(F32) + second_ref[:, k].astype(F32)
        rows_ref[:CAP, k] = here.astype(BF)
        rows_ref[CAP:, k] = there.astype(BF)
    copies = []
    for j, r in enumerate(tiles_of(out_ref.shape[0], buffer.shape[0] // 4)):
        for k in tiles_of(out_ref.shape[1], 1024):
            buffer[r, k] = dot(spread[r.start : r.start + r.size], rows_ref[:, k]).astype(BF)
        copies.append(pltpu.make_async_copy(buffer.at[r], out_ref.at[r], sem.at[j]))
        copies[j].start()
    for copy in copies:
        copy.wait()


def place(select, own, ahead, behind, first, second):
    count, width = select.shape[1], own.shape[1]
    return pl.pallas_call(
        place_kernel,
        in_specs=[IN_VMEM] * 6,
        out_specs=pl.BlockSpec(memory_space=pl.ANY),
        out_shape=jax.ShapeDtypeStruct((count, width), BF),
        scratch_shapes=[pltpu.VMEM((2 * CAP, width), BF), pltpu.VMEM((count, width), BF), pltpu.SemaphoreType.DMA((4,))],
        compiler_params=pltpu.CompilerParams(vmem_limit_bytes=8 << 20),
        name="place",
    )(*[held(x) for x in (select, own, ahead, behind, first, second)])


def per_device_ring(grad_out, layer_in, expert_ids, gate_probs, sample_ids, w_gate, w_up, w_down):
    swap = [(0, 1), (1, 0)]
    ahead, behind = ring_orders(lax.axis_size("local"))
    half = lax.axis_size("local") // 2

    def go(x):
        return lax.ppermute(x, "local", ahead)

    def back(x):
        return lax.ppermute(x, "local", behind)

    def cross(x, hops):
        count = lax.axis_size("local")
        pairs = [(i * count + a, (1 - i) * count + b) for i in (0, 1) for a, b in hops]
        return lax.ppermute(x, ("node", "local"), pairs)

    near, other, select = pick(expert_ids.T, gate_probs.T, sample_ids, grad_out, layer_in)
    far = lax.ppermute(other, "node", swap)

    weights = load(w_gate, w_up, w_down)
    saved = []
    pieces = {}

    def work_on(members, flops=0):
        outs, keep = work([rows[member] for member in members], *weights, flops)
        pieces.update(zip(members, outs))
        saved.append(keep)
        return keep[0]

    rows = {(0, 0): near, (0, 1): far}
    near_go, near_back, far_go, far_back = near, near, far, far
    for s in range(1, half):
        near_go, near_back = go(near_go), back(near_back)
        far_go, far_back = go(far_go), back(far_back)
        rows.update({(-s, 0): near_go, (s, 0): near_back, (-s, 1): far_go, (s, 1): far_back})
        if s == half - 2:
            done = work_on(list(rows)[:-2], 3000000000)
            far_go, far_back = after(far_go, done), after(far_back, done)
    near_go, near_back = together(near_go, near_back)
    far_go, far_back = together(far_go, far_back)
    last_near = jnp.concatenate([go(near_go[:CAP]), back(near_back[CAP:])])
    last_far = jnp.concatenate([go(far_go[:CAP]), back(far_back[CAP:])])
    rows.update({(half, 0): last_near, (half, 1): last_far})
    work_on([member for member in rows if member not in pieces], 0)

    def add(x, y):
        return (x.astype(F32) + y.astype(F32)).astype(BF)

    far_long, near_long = pieces[half, 1], pieces[half, 0]
    far_short, near_short = pieces[half - 1, 1], pieces[1 - half, 0]
    for s in range(half - 1, 0, -1):
        far_long, near_long = back(far_long), go(near_long)
        far_short, near_short = go(far_short), back(near_short)
        far_long, near_long = add(pieces[-s, 1], far_long), add(pieces[s, 0], near_long)
        if s > 1:
            far_short, near_short = add(pieces[s - 1, 1], far_short), add(pieces[1 - s, 0], near_short)
    saved[0] = [after(saved[0][0], far_long, near_long), *saved[0][1:]]
    grad_gate, grad_up, grad_down = weight_grads(saved)
    far_long, near_long = cross(far_long, behind), go(near_long)
    first = lax.ppermute(add(pieces[0, 1], far_short), "node", swap)
    grad_in = place(select, pieces[0, 0], near_long, near_short, first, far_long)
    return (grad_in, grad_gate, grad_up, grad_down)


def solution(mesh):
    nodes, locals_ = mesh.shape["node"], mesh.shape["local"]
    ring = nodes == 2 and locals_ % 2 == 0 and locals_ >= 8

    def per_device(*args):
        shards = FF // args[5].shape[0]
        if ring and shards == locals_:
            return per_device_ring(*args)
        return per_device_exchange(*args)

    return jax.shard_map(
        per_device,
        mesh=mesh,
        in_specs=(
            P(("groups", "node", "local"), None),
            P(("groups", "node", "local"), None),
            P(("groups", "node", "local"), None),
            P(("groups", "node", "local"), None),
            P(("groups", "node", "local"), None),
            P(("node", "local"), None),
            P(("node", "local"), None),
            P(("node", "local"), None),
        ),
        out_specs=(
            P(("groups", "node", "local"), None),
            P(("groups", "node", "local"), None),
            P(("groups", "node", "local"), None),
            P(("groups", "node", "local"), None),
        ),
        check_vma=False,
    )
```
